32 devices in a mesh: col: 8 (over z, x), gz: 4 (over y, core).
Axes of the slice: x: 2, y: 2, z: 4, core: 2. Of those that a mesh axis runs over, the one named last changes fastest.
Arguments:
- state: float32 [80, 8, 64, 128], P(None, 'gz', 'col'), may hold values from -6 to 6
- observation_site: int32 [2, 1024], replicated, may hold values from 0 to 8191
- obs_count: int32 [2, 8], P(None, 'col'), may hold values from 1 to 128, 256 in all within a row
- measured_values: float32 [2, 1024], P(None, 'col'), may hold values from -8 to 8
- observation_noise: float32 [2, 1024], P(None, 'col'), may hold values from 0.25 to 4
- loc_pattern: int32 [2, 8, 8], P(None, None, 'col'), may hold values from 0 to 1, as said below
- ocean_mask: int32 [64, 128], P('col'), may hold values 0 or 1
- zonal_current: float32 [8, 64, 128], P('gz', 'col'), may hold values from -0.45 to 0.45
Outputs:
- forecast: float32 [80, 8, 64, 128], P(None, 'gz', 'col')
The draws below stay inside these ranges and needn't reach their ends.
Inputs may be any that keep to these rules, and one draw needn't show every extreme that they name: `obs_count`: in each batch the counts sum to 256 and the largest is 128. loc_pattern[b, a, c] is 1 where a equals c and 0 where the periodic distance of a and c along the column blocks exceeds 3.
All inputs are finite; a program needn't handle non-finite values. No bound on the sum of `obs_count` or of `ocean_mask` on one device may be relied on, other than what follows from the above.
Results may differ from the reference program's by a relative error of at most 0.0003.
Values sent between devices are 32-bit elements; how exact they have to be, the bound alone decides.
No kernel may reach another device: no remote copies, remote signals or barrier semaphores. Data moves between devices by JAX's collectives and lax.ppermute only.
A program may use at most 64 MiB of HBM per device.

```python
import math
import jax
import jax.numpy as jnp
import numpy as np
from jax import lax

MEMBERS = 80
BLOCK_LONGITUDES = 8
LATITUDE_ROWS = 128
BATCH_COUNT = 2
REACH = 3
CAP = 128
DEPTH_LEVELS = 8
LON = 64
SLOT_COUNT = 1024
NOBS = 256
N_COL = 8


def draw_loc_pattern(key, part):
    key = jax.random.fold_in(key, 7)
    owner_index = jnp.arange(N_COL, dtype=jnp.int32)[:, None]
    target_index = jnp.arange(N_COL, dtype=jnp.int32)[None, :]
    spacing = (owner_index - target_index) % N_COL
    spacing = jnp.minimum(spacing, N_COL - spacing)
    coin_draw = jax.random.randint(key, (BATCH_COUNT, N_COL, N_COL), 0, 4)
    linked = (spacing <= REACH) & (coin_draw < 3)
    return jnp.where(spacing == 0, 1, jnp.where(linked, 1, 0)).astype(jnp.int32)


def place_ends(drawn, key, smallest, largest):
    shape = drawn.shape
    place = [jax.random.randint(jax.random.fold_in(key, axis), (), 0, shape[axis]) for axis in range(len(shape))]
    drawn = drawn.at[tuple(place)].set(smallest)
    longest = shape.index(max(shape))
    place[longest] = (place[longest] + 1) % shape[longest]
    return drawn.at[tuple(place)].set(largest)


def level_of(stream_key, extent, split, smallest, largest):
    def one(axis_at, shards_of):
        draws = jax.random.uniform(jax.random.fold_in(jax.random.fold_in(stream_key, 6), axis_at), (shards_of,), jnp.float32, smallest / len(split), largest / len(split))
        return jnp.repeat(jnp.exp(draws), extent[axis_at] // shards_of).reshape((-1,) + (1,) * (len(extent) - axis_at - 1))

    level = one(*split[0])
    for cut in split[1:]:
        level = level * one(*cut)
    return level


def length_profile(number_of, total, most, lean):
    loads = [(1 << 20) // math.isqrt(standing ** lean) + 1 for standing in range(2, number_of + 1)]
    surplus, holding = total - most - (number_of - 1), [1] * (number_of - 1)
    while surplus > 0:
        candidates = [i for i in range(number_of - 1) if holding[i] < most]
        pool, remaining = sum([loads[i] for i in candidates]), surplus
        for i in candidates:
            extra = min(most - holding[i], max(1, remaining * loads[i] // pool), surplus)
            holding[i] = holding[i] + extra
            surplus = surplus - extra
    return np.array([most] + holding)


def uneven(key, count, total, most, skew):
    if count == 2:
        one = jax.random.randint(key, (), max(1, total - most), min(most, total - 1) + 1)
        return jnp.stack([one, total - one])
    tallies = jnp.asarray(length_profile(count, total, most, skew), jnp.int32)
    pairs = (count - 1) // 2
    giver, taker = tallies[1:1 + 2 * pairs:2], tallies[2:2 + 2 * pairs:2]
    margin = jnp.minimum(giver - 1, most - taker)
    moved = jax.random.randint(jax.random.fold_in(key, 1), (pairs,), 0, 1 << 20) % (margin + 1)
    tallies = tallies.at[1:1 + 2 * pairs:2].set(giver - moved).at[2:2 + 2 * pairs:2].set(taker + moved)
    return tallies[jax.random.permutation(jax.random.fold_in(key, 2), count)]


def scatter_about(stream_key, extent, deviation, reach, pieces=(), kind=jnp.bfloat16):
    entries = jax.random.normal(stream_key, extent, jnp.float32) * deviation
    if len(pieces) > 0:
        entries = level_of(stream_key, extent, pieces, -0.22, 0.18) * entries
    return jnp.clip(entries, min=-reach, max=reach).astype(kind)


def setup_inputs(seed: int = 0) -> dict:
    streams_of = jax.random.split(jax.random.key(seed), 9)
    return {
        "state": scatter_about(streams_of[0], (MEMBERS, DEPTH_LEVELS, LON, LATITUDE_ROWS), 1.0, 6.0, ((1, 4), (2, 8)), jnp.float32),
        "observation_site": place_ends(jax.random.randint(streams_of[1], (BATCH_COUNT, SLOT_COUNT), 0, DEPTH_LEVELS * BLOCK_LONGITUDES * LATITUDE_ROWS), jax.random.fold_in(streams_of[1], 1), 0, (DEPTH_LEVELS * BLOCK_LONGITUDES * LATITUDE_ROWS) - 1).astype(jnp.int32),
        "obs_count": jax.vmap(lambda own: uneven(own, N_COL, NOBS, CAP, 2))(jax.random.split(streams_of[2], BATCH_COUNT)).reshape((BATCH_COUNT, N_COL)).astype(jnp.int32),
        "measured_values": scatter_about(streams_of[3], (BATCH_COUNT, SLOT_COUNT), 1.5, 8.0, ((1, 8),), jnp.float32),
        "observation_noise": jnp.clip(jnp.exp(math.log(4.0) - 2.7725887 * jax.random.uniform(streams_of[4], (BATCH_COUNT, SLOT_COUNT), jnp.float32) ** level_of(streams_of[4], (BATCH_COUNT, SLOT_COUNT), ((1, 8),), -0.2, 0.2)), 0.25, 4.0),
        "loc_pattern": draw_loc_pattern(jax.random.fold_in(streams_of[8], 71), 0),
        "ocean_mask": place_ends((jax.random.randint(streams_of[6], (LON, LATITUDE_ROWS), 0, 8) < 7).astype(jnp.int32), jax.random.fold_in(streams_of[6], 1), 0, 1),
        "zonal_current": jnp.clip(jax.random.uniform(streams_of[7], (DEPTH_LEVELS, LON, LATITUDE_ROWS), jnp.float32, -0.45, 0.45) * level_of(streams_of[7], (DEPTH_LEVELS, LON, LATITUDE_ROWS), ((0, 4), (1, 8)), -0.4, 0.0), -0.45, 0.45),
    }


PRECISE = lax.Precision.HIGHEST
lateral_mix = 0.2
vertical_mix = 0.15

def prior_terms(prior_ens, obs_values, obs_errors):
    ens_mean = lax.optimization_barrier(jnp.mean(prior_ens, axis=0))
    anomaly = prior_ens - ens_mean
    spread = lax.optimization_barrier(jnp.sum(anomaly * anomaly, axis=0)) / (prior_ens.shape[0] - 1)
    variance_sum = spread + obs_errors
    shrink = 1.0 / (1.0 + jnp.sqrt(obs_errors / variance_sum))
    gain_coef = (obs_values - ens_mean) / variance_sum - shrink * anomaly / variance_sum
    return (anomaly, gain_coef)

def slot_places(owner_cells, owner_block):
    obs_lev = owner_cells // (BLOCK_LONGITUDES * LATITUDE_ROWS)
    obs_lon = owner_block * BLOCK_LONGITUDES + owner_cells // LATITUDE_ROWS % BLOCK_LONGITUDES
    obs_lat = owner_cells % LATITUDE_ROWS
    return (obs_lev, obs_lon, obs_lat)

def taper_block(lev_cells, lon_cells, obs_lev, obs_lon, obs_lat, lon_all):
    lon_gap = jnp.abs(lon_cells[:, None] - obs_lon[None, :])
    lon_gap = jnp.minimum(lon_gap, lon_all - lon_gap).astype(jnp.float32) / (2.0 * BLOCK_LONGITUDES)
    lat_cells = jnp.arange(LATITUDE_ROWS).astype(jnp.int32)
    lat_gap = (lat_cells[:, None] - obs_lat[None, :]).astype(jnp.float32) / (LATITUDE_ROWS // 8)
    lev_gap = (lev_cells[:, None] - obs_lev[None, :]).astype(jnp.float32) / 2.0
    lon_taper = 1.0 / (1.0 + lon_gap * lon_gap)
    lat_taper = 1.0 / (1.0 + lat_gap * lat_gap)
    lev_taper = 1.0 / (1.0 + lev_gap * lev_gap)
    return lev_taper[:, None, None, :] * lon_taper[None, :, None, :] * lat_taper[None, None, :, :]

def analyse(ensemble_fields, batch_index, observation_site, obs_count, measured_values, observation_noise, loc_pattern, marine_float_kind):
    slots = jnp.arange(N_COL * CAP).astype(jnp.int32)
    holder_entire = slots // CAP
    occupied = (slots % CAP < obs_count[batch_index][holder_entire]).astype(jnp.float32)
    obs_lev, obs_lon, obs_lat = slot_places(observation_site[batch_index], holder_entire)
    prior_ens = ensemble_fields[:, obs_lev, obs_lon, obs_lat] * occupied
    anomaly, gain_coef = prior_terms(prior_ens, measured_values[batch_index], observation_noise[batch_index])
    mean_removed = ensemble_fields - lax.optimization_barrier(jnp.mean(ensemble_fields, axis=0))
    lev_cells = jnp.arange(DEPTH_LEVELS).astype(jnp.int32)

    def column_block(col_block):
        block_ens = lax.dynamic_slice_in_dim(mean_removed, col_block * BLOCK_LONGITUDES, BLOCK_LONGITUDES, 2)
        lon_cells = col_block * BLOCK_LONGITUDES + jnp.arange(BLOCK_LONGITUDES).astype(jnp.int32)

        def visit(running, owner_block):
            weight = loc_pattern[batch_index, owner_block, col_block]

            def active(partial_sum):
                start = owner_block * CAP
                part_anom = lax.dynamic_slice_in_dim(anomaly, start, CAP, 1)
                part_gain = lax.dynamic_slice_in_dim(gain_coef, start, CAP, 1)
                part_lev = lax.dynamic_slice_in_dim(obs_lev, start, CAP, 0)
                part_lon = lax.dynamic_slice_in_dim(obs_lon, start, CAP, 0)
                part_lat = lax.dynamic_slice_in_dim(obs_lat, start, CAP, 0)
                localize = weight.astype(jnp.float32) * taper_block(lev_cells, lon_cells, part_lev, part_lon, part_lat, LON)
                covariance = jnp.einsum('mvxy,mk->vxyk', block_ens, part_anom, precision=PRECISE) / (MEMBERS - 1)
                return partial_sum + jnp.einsum('mk,vxyk->mvxy', part_gain, covariance * localize, precision=PRECISE)
            return (lax.cond(weight != 0, active, lambda partial_sum: partial_sum, running), None)
        zero_block = jnp.zeros(block_ens.shape, jnp.float32)
        result, unused = lax.scan(visit, zero_block, jnp.arange(N_COL).astype(jnp.int32))
        return result
    blocks = lax.map(column_block, jnp.arange(N_COL).astype(jnp.int32))
    increment = jnp.moveaxis(blocks, 0, 2).reshape(ensemble_fields.shape)
    return ensemble_fields + marine_float_kind * increment

def predict_next_interval(posterior_ensemble, zonal_current, marine_float_kind):
    lon_next = jnp.roll(posterior_ensemble, -1, axis=2)
    lon_prev = jnp.roll(posterior_ensemble, 1, axis=2)
    lat_pad = jnp.pad(posterior_ensemble, ((0, 0), (0, 0), (0, 0), (1, 1)))
    lat_next = lat_pad[..., 2:]
    lat_prev = lat_pad[..., :-2]
    lev_pad = jnp.pad(posterior_ensemble, ((0, 0), (1, 1), (0, 0), (0, 0)))
    lev_next = lev_pad[:, 2:]
    lev_prev = lev_pad[:, :-2]
    tendency = -0.5 * zonal_current * (lon_next - lon_prev) + lateral_mix * (lon_next + lon_prev + lat_next + lat_prev - 4.0 * posterior_ensemble) + vertical_mix * (lev_next + lev_prev - 2.0 * posterior_ensemble)
    return posterior_ensemble + marine_float_kind * tendency

def reference(state, observation_site, obs_count, measured_values, observation_noise, loc_pattern, ocean_mask, zonal_current):
    marine_float_kind = ocean_mask.astype(jnp.float32)
    ensemble_fields = state
    for batch_index in range(BATCH_COUNT):
        ensemble_fields = analyse(ensemble_fields, batch_index, observation_site, obs_count, measured_values, observation_noise, loc_pattern, marine_float_kind)
    return predict_next_interval(ensemble_fields, zonal_current, marine_float_kind)
```

```python
import functools

import jax
import jax.numpy as jnp
from jax import lax
from jax.experimental import pallas as pl
from jax.experimental.pallas import tpu as pltpu
from jax.sharding import PartitionSpec as P

LEVS = 2
LONS = 8
LATS = 128
BATCHES = 2
REACH = 3
CAP = 128
MEAN_COUNT = 32
WINDOW = 2 * REACH + 1
CHUNK = 256

CELLS = LEVS * LONS * LATS
ROWS = LEVS * LONS
CORE_ROW = 16
Y_ROW = 24
WEST_ROW = 32
EAST_ROW = 34
EXT_ROWS = 36

LATERAL_MIX = 0.2
VERTICAL_MIX = 0.15

F32 = jnp.float32
BF16 = jnp.bfloat16


def iota(shape, dim):
    return lax.broadcasted_iota(jnp.int32, shape, dim)


def halves(x):
    high = x.astype(BF16)
    return high, (x - high.astype(F32)).astype(BF16)


def dot(a, b):
    return lax.dot_general(a, b, (((1,), (0,)), ((), ())), preferred_element_type=F32)


def dot_lanes(a, b):
    return lax.dot_general(a, b, (((1,), (1,)), ((), ())), preferred_element_type=F32)


def for_each(count, body):
    if count == 1:
        body(0)
    else:
        lax.fori_loop(0, count, lambda i, unused: (body(i), unused)[1], 0)


def rows_of(members):
    names = ("mask", "value", "noise", "links", "site", "occupied", "owner", "count")
    return {name: members + i for i, name in enumerate(names)}


def pick_kernel(members, scal, site, value, noise, links, mask, state, out):
    col, gz = scal[0], scal[1]
    lane = iota((1, CAP), 1)
    index, filled = [], []
    for b in range(BATCHES):
        occupied = lane < scal[2 + b]
        filled.append(occupied)
        at = pl.multiple_of(col * CAP, CAP)
        index.append(jnp.where(occupied, site[b : b + 1, pl.ds(at, CAP)] - gz * CELLS, -1))
    wanted = jnp.concatenate(index, 1)
    total = jnp.zeros((3 * members + 16, BATCHES * CAP), F32)
    cell = iota((2 * LATS, BATCHES * CAP), 0)
    for pair in range(ROWS // 2):
        left = []
        for r in (2 * pair, 2 * pair + 1):
            x = state[pl.ds(r, members, stride=ROWS), :]
            high = x.astype(BF16)
            rest = x - high.astype(F32)
            middle = rest.astype(BF16)
            low = (rest - middle.astype(F32)).astype(BF16)
            lon = r % LONS
            ocean = jnp.broadcast_to(mask[lon : lon + 1, :], (16, LATS)).astype(BF16)
            left.append(jnp.concatenate([high, ocean, middle, low], 0))
        hit = jnp.where(cell + pair * 2 * LATS == wanted, 1.0, 0.0).astype(BF16)
        total = total + dot(jnp.concatenate(left, 1), hit)
    m = members
    picked = (total[:m] + total[m + 16 : 2 * m + 16]) + total[2 * m + 16 :]
    first = jnp.where(gz == 0, 1.0, 0.0)
    for b in range(BATCHES):
        here = slice(b * CAP, (b + 1) * CAP)
        once = jnp.where(filled[b], first, 0.0)
        at = pl.multiple_of(col * CAP, CAP)
        out[b, :m, :] = picked[:, here]
        tail = [
            total[m : m + 1, here],
            value[b : b + 1, :] * once,
            noise[b : b + 1, :] * once,
            links[b : b + 1, :] * first,
            site[b : b + 1, pl.ds(at, CAP)].astype(F32) * once,
            once,
            once * col.astype(F32),
            jnp.full((1, CAP), scal[2 + b].astype(F32) * first),
        ]
        out[b, m:, :] = jnp.concatenate(tail, 0)


def step_kernel(
    members, blocks, columns, around, chunks,
    scal, mine, other, state, core_edge, y_edge, west, east, mask, zonal, out,
    packed, fields, gained,
):
    col, gz = scal[0], scal[1]
    odd = gz % 2
    lon_all = columns * LONS
    place = rows_of(members)
    denominator = 1.0 / (members - 1)
    height = members + 8
    owners = [col ^ j if around is None else (col + around[j] + columns) % columns for j in range(blocks)]

    links = []
    packed[...] = jnp.zeros_like(packed)
    for b in range(BATCHES):
        start = 0
        own_links = []
        for j in range(blocks):
            block = jnp.where(odd == b, mine[j], other[j])
            own_links.append(block[place["links"] : place["links"] + 1, :])
            tall = jnp.concatenate([block, jnp.zeros((LATS - height, CAP), F32)], 0)
            packed[b, pl.ds(start, CAP), :] = tall.T
            start = start + block[place["count"], 0].astype(jnp.int32)
        links.append(own_links)

    for r in range(ROWS):
        fields[r] = state[pl.ds(r, members, stride=ROWS), :]
    for lon in range(LONS):
        fields[CORE_ROW + lon] = core_edge[pl.ds(lon, members, stride=LONS), :]
        fields[Y_ROW + lon] = y_edge[pl.ds(lon, members, stride=LONS), :]
    for lev in range(LEVS):
        fields[WEST_ROW + lev] = west[pl.ds(lev, members, stride=LEVS), :]
        fields[EAST_ROW + lev] = east[pl.ds(lev, members, stride=LEVS), :]
    ocean = [mask[lon : lon + 1, :] for lon in range(LONS)] * 4
    ocean += [west[members * LEVS : members * LEVS + 1, :]] * LEVS
    ocean += [east[members * LEVS : members * LEVS + 1, :]] * LEVS

    lane = iota((1, LATS), 1)
    own = lane < ROWS
    near = (lane >= CORE_ROW) & (lane < Y_ROW)
    far = (lane >= Y_ROW) & (lane < WEST_ROW)
    above, below = LEVS * gz + LEVS, LEVS * gz - 1
    row_lev = LEVS * gz + jnp.where(own, lane // LONS, lane % LEVS)
    row_lev = jnp.where(near, jnp.where(odd == 0, above, below), row_lev)
    row_lev = jnp.where(far, jnp.where(odd == 0, below, above), row_lev)
    west_lon = (col * LONS + lon_all - 1) % lon_all
    east_lon = (col * LONS + LONS) % lon_all
    row_lon = jnp.where(
        lane < WEST_ROW, col * LONS + lane % LONS, jnp.where(lane < EAST_ROW, west_lon, east_lon)
    )
    west_col = (col + columns - 1) % columns
    east_col = (col + 1) % columns

    def links_of(b, target):
        row = jnp.zeros((1, CAP), F32)
        for j in range(blocks):
            row = row + jnp.where(owners[j] == target, links[b][j], 0.0)
        return row

    def places(site, owner):
        site = site.astype(jnp.int32)
        lev = site // (LONS * LATS)
        lon = owner.astype(jnp.int32) * LONS + site // LATS % LONS
        return lev.astype(F32), lon.astype(F32), (site % LATS).astype(F32)

    def lon_square(a, b):
        gap = jnp.abs(a - b)
        gap = jnp.minimum(gap, lon_all - gap) * (1.0 / (2.0 * LONS))
        return 1.0 + gap * gap

    def lev_square(a, b):
        gap = (a - b) * 0.5
        return 1.0 + gap * gap

    def lat_square(a, b):
        gap = (a - b) * (1.0 / (LATS // 8))
        return 1.0 + gap * gap

    def slots_of(b, k):
        start = k * CHUNK if isinstance(k, int) else pl.multiple_of(k * CHUNK, CHUNK)
        tall = packed[b, pl.ds(start, CHUNK), :]
        return tall, tall.T

    def centred_parts(x):
        x = x - jnp.sum(x, 0, keepdims=True) * (1.0 / members)
        high, low = halves(x)
        return jnp.concatenate([high, low, high, jnp.zeros((16, x.shape[1]), BF16)], 0)

    def batch_terms(b, k):
        tall, wide = slots_of(b, k)
        occupied = wide[place["occupied"] : place["occupied"] + 1]
        if b == 0:
            prior = wide[:members]
        else:
            prior = jnp.concatenate([fields[EXT_ROWS + 2 * k], fields[EXT_ROWS + 2 * k + 1]], 1) * occupied
        value = wide[place["value"] : place["value"] + 1]
        noise = jnp.where(occupied > 0, wide[place["noise"] : place["noise"] + 1], 1.0)
        mean = jnp.sum(prior, 0, keepdims=True) / members
        anomaly = prior - mean
        spread = jnp.sum(anomaly * anomaly, 0, keepdims=True) * denominator
        total = spread + noise
        shrink = 1.0 / (1.0 + jnp.sqrt(noise / total))
        gain = ((value - mean) - shrink * anomaly) / total
        high = anomaly.astype(BF16).astype(F32)
        sides = jnp.concatenate([high, high, anomaly - high, jnp.zeros((16, CHUNK), F32)], 0)
        sides = sides.T.astype(BF16)
        gain_high, gain_low = halves(gain)
        gains = jnp.concatenate([gain_high, gain_low], 0)

        def column(name):
            return tall[:, place[name] : place[name] + 1]

        lev, lon, lat = places(column("site"), column("owner"))
        holder = jnp.where(lane.astype(F32) == column("owner"), 1.0, 0.0)
        weight = jnp.where(
            lane < WEST_ROW,
            jnp.sum(holder * links_of(b, col), 1, keepdims=True),
            jnp.where(
                lane < EAST_ROW,
                jnp.sum(holder * links_of(b, west_col), 1, keepdims=True),
                jnp.sum(holder * links_of(b, east_col), 1, keepdims=True),
            ),
        )
        row_part = weight * denominator / (
            lev_square(row_lev.astype(F32), lev) * lon_square(row_lon.astype(F32), lon)
        )
        lat_part = 1.0 / lat_square(lane.astype(F32), lat)
        return sides, gains, row_part, lat_part, (lev, lon, lat, holder)

    def increment(x, sides, gains, local):
        weighted = dot(sides, centred_parts(x)) * local
        high, low = halves(weighted)
        first = dot(gains, high)
        return (first[:members] + first[members:]) + dot(gains[:members], low)

    def site_weights(where0, k1):
        lev0, lon0, lat0, holder = where0
        tall, wide = slots_of(1, k1)
        owner = wide[place["owner"] : place["owner"] + 1]
        lev, lon, lat = places(wide[place["site"] : place["site"] + 1], owner)
        pad = (-blocks) % 16
        spare = [jnp.zeros((pad, CAP), F32)] if pad else []
        table = jnp.concatenate(links[0] + spare, 0).astype(BF16)
        by_block = dot_lanes(holder.astype(BF16), table).astype(BF16)
        spare = [jnp.zeros((pad, CHUNK), F32)] if pad else []
        there = [jnp.where(owner == owners[j].astype(F32), 1.0, 0.0) for j in range(blocks)]
        weight = dot(by_block, jnp.concatenate(there + spare, 0).astype(BF16))
        square = lat_square(lat0, lat) * lon_square(lon0, lon) * lev_square(lev0, lev)
        return weight * denominator / square, wide

    direct = chunks == 1

    def analyse(b):
        if not direct:
            gained[...] = jnp.zeros_like(gained)

        def chunk(k):
            sides, gains, row_part, lat_part, where = batch_terms(b, k)
            if b == 0:

                def site_chunk(k1):
                    local, wide = site_weights(where, k1)
                    x = wide[:members]
                    moved = increment(x, sides, gains, local) * wide[members : members + 1]
                    for h in range(2):
                        at = EXT_ROWS + 2 * k1 + h
                        piece = slice(h * LATS, (h + 1) * LATS)
                        if direct:
                            fields[at] = x[:, piece] + moved[:, piece]
                        else:
                            before = jnp.where(k == 0, x[:, piece], fields[at])
                            fields[at] = before + moved[:, piece]

                for_each(chunks, site_chunk)
            for r in range(0, EXT_ROWS, 2):
                x = jnp.concatenate([fields[r], fields[r + 1]], 1)
                local = jnp.concatenate(
                    [lat_part * row_part[:, r : r + 1], lat_part * row_part[:, r + 1 : r + 2]], 1
                )
                moved = increment(x, sides, gains, local)
                moved = moved * jnp.concatenate([ocean[r], ocean[r + 1]], 1)
                for h in range(2):
                    piece = slice(h * LATS, (h + 1) * LATS)
                    if direct:
                        fields[r + h] = x[:, piece] + moved[:, piece]
                    else:
                        gained[r + h] = gained[r + h] + moved[:, piece]

        for_each(chunks, chunk)
        if not direct:
            for r in range(EXT_ROWS):
                fields[r] = fields[r] + gained[r]

    for b in range(BATCHES):
        analyse(b)

    lower = jnp.where(odd == 0, Y_ROW, CORE_ROW)
    upper = jnp.where(odd == 0, CORE_ROW, Y_ROW)
    for r in range(ROWS):
        lev, lon = r // LONS, r % LONS
        x = fields[r]
        lon_next = fields[r + 1] if lon < LONS - 1 else fields[EAST_ROW + lev]
        lon_prev = fields[r - 1] if lon > 0 else fields[WEST_ROW + lev]
        lat_next = jnp.where(lane < LATS - 1, pltpu.roll(x, LATS - 1, 1), 0.0)
        lat_prev = jnp.where(lane > 0, pltpu.roll(x, 1, 1), 0.0)
        vertical = fields[r ^ LONS] + fields[(lower if lev == 0 else upper) + lon]
        tendency = (
            -0.5 * zonal[r : r + 1, :] * (lon_next - lon_prev)
            + LATERAL_MIX * (lon_next + lon_prev + lat_next + lat_prev - 4.0 * x)
            + VERTICAL_MIX * (vertical - 2.0 * x)
        )
        out[pl.ds(r, members, stride=ROWS), :] = x + ocean[lon] * tendency


def swapped(x, axis, bit):
    return lax.ppermute(x, axis, [(i, i ^ bit) for i in range(lax.axis_size(axis))])


def shifted(x, axis, by):
    count = lax.axis_size(axis)
    return lax.ppermute(x, axis, [(i, (i + by) % count) for i in range(count)])


def local(state, observation_site, obs_count, measured_values, observation_noise, loc_pattern, ocean_mask, zonal_current):
    members = state.shape[0]
    columns = lax.axis_size("col")
    floors = lax.axis_size("gz")
    col = lax.axis_index("col").astype(jnp.int32)
    gz = lax.axis_index("gz").astype(jnp.int32)
    core = gz % 2
    vmem = pl.BlockSpec(memory_space=pltpu.VMEM)
    smem = pl.BlockSpec(memory_space=pltpu.SMEM)
    height = members + 8

    mask = ocean_mask.astype(F32)
    flat = state.reshape(members * ROWS, LATS)
    scal = jnp.stack([col, gz, obs_count[0, 0], obs_count[1, 0]])
    links = jnp.pad(loc_pattern[:, :, 0].astype(F32), ((0, 0), (0, CAP - columns)))

    payload = pl.pallas_call(
        functools.partial(pick_kernel, members),
        out_shape=jax.ShapeDtypeStruct((BATCHES, height, CAP), F32),
        in_specs=[smem] + [vmem] * 6,
        out_specs=vmem,
        name="pick_priors",
    )(scal, observation_site, measured_values, observation_noise, links, mask, flat)

    core_edge = swapped(lax.dynamic_index_in_dim(state, 1 - core, 1, False), "gz", 1)
    ends = [(i, i + 1) for i in range(1, floors - 1, 2)]
    y_edge = lax.ppermute(
        lax.dynamic_index_in_dim(state, core, 1, False), "gz", ends + [(j, i) for i, j in ends]
    )
    lon_edges = []
    for lon, by in ((LONS - 1, 1), (0, -1)):
        edge = jnp.concatenate(
            [state[:, :, lon, :].reshape(members * LEVS, LATS), jnp.broadcast_to(mask[lon : lon + 1], (8, LATS))], 0
        )
        lon_edges.append(shifted(edge, "col", by))
    west, east = lon_edges

    mine = lax.dynamic_index_in_dim(payload, core, 0, False)
    given = lax.dynamic_index_in_dim(payload, 1 - core, 0, False)
    mine = mine + swapped(given, "gz", 1)
    bit = 2
    while bit < floors:
        mine = mine + swapped(mine, "gz", bit)
        bit *= 2
    if columns <= 2 * WINDOW + 1 and columns & (columns - 1) == 0:
        around = None
        pair = jnp.stack([mine, swapped(mine, "col", 1)])
        gathered = jnp.concatenate([pair] + [swapped(pair, "col", bit) for bit in range(2, columns, 2)])
    else:
        reach = min(WINDOW, (columns - 1) // 2)
        around = tuple(range(-reach, columns - reach)) if columns <= 2 * WINDOW + 1 else tuple(range(-WINDOW, WINDOW + 1))
        gathered = jnp.stack([mine if by == 0 else shifted(mine, "col", -by) for by in around])
    blocks = gathered.shape[0]
    other = swapped(gathered, "gz", 1)

    slots = min(blocks * CAP, MEAN_COUNT * columns)
    chunks = -(-slots // CHUNK)
    rows = EXT_ROWS + 2 * chunks
    out = pl.pallas_call(
        functools.partial(step_kernel, members, blocks, columns, around, chunks),
        out_shape=jax.ShapeDtypeStruct((members * ROWS, LATS), F32),
        in_specs=[smem] + [vmem] * 9,
        out_specs=vmem,
        scratch_shapes=[
            pltpu.VMEM((BATCHES, chunks * CHUNK + CAP, CAP), F32),
            pltpu.VMEM((rows, members, LATS), F32),
            pltpu.VMEM((EXT_ROWS if chunks > 1 else 1, members, LATS), F32),
        ],
        compiler_params=pltpu.CompilerParams(vmem_limit_bytes=48 * 1024 * 1024),
        name="analyse_and_step",
    )(
        scal,
        gathered,
        other,
        flat,
        core_edge.reshape(members * LONS, LATS),
        y_edge.reshape(members * LONS, LATS),
        west,
        east,
        mask,
        zonal_current.reshape(ROWS, LATS),
    )
    return out.reshape(state.shape)


def solution(mesh):
    in_specs = (
        P(None, "gz", "col", None),
        P(),
        P(None, "col"),
        P(None, "col"),
        P(None, "col"),
        P(None, None, "col"),
        P("col", None),
        P("gz", "col", None),
    )
    out_specs = P(None, "gz", "col", None)
    return jax.shard_map(local, mesh=mesh, in_specs=in_specs, out_specs=out_specs, check_vma=False)
```

```python
import functools

import jax
import jax.numpy as jnp
from jax import lax
from jax.experimental import pallas as pl
from jax.experimental.pallas import tpu as pltpu
from jax.sharding import PartitionSpec as P

LEVS = 2
LONS = 8
LATS = 128
BATCHES = 2
REACH = 3
CAP = 128
MEAN_COUNT = 32
WINDOW = 2 * REACH + 1
CHUNK = 256

CELLS = LEVS * LONS * LATS
ROWS = LEVS * LONS
CORE_ROW = 16
Y_ROW = 24
INNER_ROW = 32
OUTER_ROW = 34
EXT_ROWS = 36

LATERAL_MIX = 0.2
VERTICAL_MIX = 0.15

F32 = jnp.float32
BF16 = jnp.bfloat16


def iota(shape, dim):
    return lax.broadcasted_iota(jnp.int32, shape, dim)


def halves(x):
    high = x.astype(BF16)
    return high, (x - high.astype(F32)).astype(BF16)


def dot(a, b):
    return lax.dot_general(a, b, (((1,), (0,)), ((), ())), preferred_element_type=F32)


def dot_lanes(a, b):
    return lax.dot_general(a, b, (((1,), (1,)), ((), ())), preferred_element_type=F32)


def for_each(count, body):
    if count == 1:
        body(0)
    else:
        lax.fori_loop(0, count, lambda i, unused: (body(i), unused)[1], 0)


def rows_of(members):
    names = ("mask", "value", "noise", "links", "site", "occupied", "owner", "count")
    return {name: members + i for i, name in enumerate(names)}


def position():
    return lax.axis_index("col").astype(jnp.int32), lax.axis_index("gz").astype(jnp.int32)


def pick_kernel(members, columns, count, linked, site, value, noise, mask, state, kept, core_send, y_send, inner, outer):
    col, gz = position()
    core = gz % 2
    lane = iota((1, CAP), 1)
    at = pl.multiple_of(col * CAP, CAP)
    index, filled = [], []
    for b in range(BATCHES):
        occupied = lane < count[b, 0]
        filled.append(occupied)
        index.append(jnp.where(occupied, site[b : b + 1, pl.ds(at, CAP)] - gz * CELLS, -1))
    wanted = jnp.concatenate(index, 1)
    total = jnp.zeros((3 * members + 16, BATCHES * CAP), F32)
    cell = iota((2 * LATS, BATCHES * CAP), 0)
    ocean = mask[...].astype(F32)
    for pair in range(ROWS // 2):
        left = []
        for r in (2 * pair, 2 * pair + 1):
            x = state[pl.ds(r, members, stride=ROWS), :]
            high = x.astype(BF16)
            rest = x - high.astype(F32)
            middle = rest.astype(BF16)
            low = (rest - middle.astype(F32)).astype(BF16)
            lon = r % LONS
            row = jnp.broadcast_to(ocean[lon : lon + 1, :], (16, LATS)).astype(BF16)
            left.append(jnp.concatenate([high, row, middle, low], 0))
        hit = jnp.where(cell + pair * 2 * LATS == wanted, 1.0, 0.0).astype(BF16)
        total = total + dot(jnp.concatenate(left, 1), hit)
    m = members
    height = m + 8
    picked = (total[:m] + total[m + 16 : 2 * m + 16]) + total[2 * m + 16 :]
    first = jnp.where(gz == 0, 1.0, 0.0)
    for b in range(BATCHES):
        here = slice(b * CAP, (b + 1) * CAP)
        once = jnp.where(filled[b], first, 0.0)
        links = jnp.zeros((1, CAP), F32)
        for a in range(columns):
            links = jnp.where(lane == a, linked[b, a, 0].astype(F32), links)
        tail = [
            total[m : m + 1, here],
            value[b : b + 1, :] * once,
            noise[b : b + 1, :] * once,
            links * first,
            site[b : b + 1, pl.ds(at, CAP)].astype(F32) * once,
            once,
            once * col.astype(F32),
            jnp.full((1, CAP), count[b, 0].astype(F32) * first),
        ]
        block = jnp.concatenate([picked[:, here]] + tail, 0)

        @pl.when(core == b)
        def _():
            kept[...] = block

        @pl.when(core != b)
        def _():
            core_send[:height, :] = block

    for member in range(members):
        up = state[pl.ds(pl.multiple_of(member * ROWS + (1 - core) * LONS, LONS), LONS), :]
        core_send[height + member * LONS : height + (member + 1) * LONS, :] = up
        down = state[pl.ds(pl.multiple_of(member * ROWS + core * LONS, LONS), LONS), :]
        y_send[member * LONS : (member + 1) * LONS, :] = down
    even = col % 2 == 0
    for lev in range(LEVS):
        west = state[pl.ds(lev * LONS, members, stride=ROWS), :]
        east = state[pl.ds(lev * LONS + LONS - 1, members, stride=ROWS), :]
        inner[lev * members : (lev + 1) * members, :] = jnp.where(even, east, west)
        outer[lev * members : (lev + 1) * members, :] = jnp.where(even, west, east)
    west = jnp.broadcast_to(ocean[:1], (8, LATS))
    east = jnp.broadcast_to(ocean[LONS - 1 :], (8, LATS))
    inner[LEVS * members :, :] = jnp.where(even, east, west)
    outer[LEVS * members :, :] = jnp.where(even, west, east)


def step_kernel(
    members, parts, columns, around, chunks, mask, zonal, state, core_edge, y_edge, inner, outer, *rest
):
    mine_parts, other_parts = rest[: len(parts)], rest[len(parts) : 2 * len(parts)]
    out, packed, fields, gained = rest[2 * len(parts) :]
    mine = [part.at[i] for part, size in zip(mine_parts, parts) for i in range(size)]
    other = [part.at[i] for part, size in zip(other_parts, parts) for i in range(size)]
    blocks = len(mine)
    col, gz = position()
    odd = gz % 2
    even_col = col % 2 == 0
    lon_all = columns * LONS
    place = rows_of(members)
    denominator = 1.0 / (members - 1)
    height = members + 8
    owners = [col ^ j if around is None else (col + around[j] + columns) % columns for j in range(blocks)]

    inner_start = inner.shape[0] - (members * LEVS + 8)
    links = []
    packed[...] = jnp.zeros_like(packed)
    for b in range(BATCHES):
        start = 0
        own_links = []
        for j in range(blocks):
            block = jnp.where(odd == b, mine[j][:height, :], other[j][:height, :])
            own_links.append(block[place["links"] : place["links"] + 1, :])
            tall = jnp.concatenate([block, jnp.zeros((LATS - height, CAP), F32)], 0)
            packed[b, pl.ds(start, CAP), :] = tall.T
            start = start + block[place["count"], 0].astype(jnp.int32)
        links.append(own_links)

    for r in range(ROWS):
        fields[r] = state[pl.ds(r, members, stride=ROWS), :]
    for lon in range(LONS):
        fields[CORE_ROW + lon] = core_edge[pl.ds(height + lon, members, stride=LONS), :]
        fields[Y_ROW + lon] = y_edge[pl.ds(lon, members, stride=LONS), :]
    for lev in range(LEVS):
        inner_at, outer_at = inner_start + lev * members, lev * members
        fields[INNER_ROW + lev] = inner[inner_at : inner_at + members, :]
        fields[OUTER_ROW + lev] = outer[outer_at : outer_at + members, :]
    dry = mask[...].astype(F32)
    ocean = [dry[lon : lon + 1] for lon in range(LONS)] * 4
    edge = members * LEVS
    ocean += [inner[inner_start + edge : inner_start + edge + 1, :]] * LEVS
    ocean += [outer[edge : edge + 1, :]] * LEVS

    lane = iota((1, LATS), 1)
    own = lane < ROWS
    near = (lane >= CORE_ROW) & (lane < Y_ROW)
    far = (lane >= Y_ROW) & (lane < INNER_ROW)
    above, below = LEVS * gz + LEVS, LEVS * gz - 1
    row_lev = LEVS * gz + jnp.where(own, lane // LONS, lane % LEVS)
    row_lev = jnp.where(near, jnp.where(odd == 0, above, below), row_lev)
    row_lev = jnp.where(far, jnp.where(odd == 0, below, above), row_lev)
    west_lon = (col * LONS + lon_all - 1) % lon_all
    east_lon = (col * LONS + LONS) % lon_all
    inner_lon = jnp.where(even_col, east_lon, west_lon)
    outer_lon = jnp.where(even_col, west_lon, east_lon)
    row_lon = jnp.where(
        lane < INNER_ROW, col * LONS + lane % LONS, jnp.where(lane < OUTER_ROW, inner_lon, outer_lon)
    )
    west_col = (col + columns - 1) % columns
    east_col = (col + 1) % columns
    inner_col = jnp.where(even_col, east_col, west_col)
    outer_col = jnp.where(even_col, west_col, east_col)

    def links_of(b, target):
        row = jnp.zeros((1, CAP), F32)
        for j in range(blocks):
            row = row + jnp.where(owners[j] == target, links[b][j], 0.0)
        return row

    def places(site, owner):
        site = site.astype(jnp.int32)
        lev = site // (LONS * LATS)
        lon = owner.astype(jnp.int32) * LONS + site // LATS % LONS
        return lev.astype(F32), lon.astype(F32), (site % LATS).astype(F32)

    def lon_square(a, b):
        gap = jnp.abs(a - b)
        gap = jnp.minimum(gap, lon_all - gap) * (1.0 / (2.0 * LONS))
        return 1.0 + gap * gap

    def lev_square(a, b):
        gap = (a - b) * 0.5
        return 1.0 + gap * gap

    def lat_square(a, b):
        gap = (a - b) * (1.0 / (LATS // 8))
        return 1.0 + gap * gap

    def slots_of(b, k):
        start = k * CHUNK if isinstance(k, int) else pl.multiple_of(k * CHUNK, CHUNK)
        tall = packed[b, pl.ds(start, CHUNK), :]
        return tall, tall.T

    def centred_parts(x):
        x = x - jnp.sum(x, 0, keepdims=True) * (1.0 / members)
        high, low = halves(x)
        return jnp.concatenate([high, low, high, jnp.zeros((16, x.shape[1]), BF16)], 0)

    def batch_terms(b, k):
        tall, wide = slots_of(b, k)
        occupied = wide[place["occupied"] : place["occupied"] + 1]
        if b == 0:
            prior = wide[:members]
        else:
            prior = jnp.concatenate([fields[EXT_ROWS + 2 * k], fields[EXT_ROWS + 2 * k + 1]], 1) * occupied
        value = wide[place["value"] : place["value"] + 1]
        noise = jnp.where(occupied > 0, wide[place["noise"] : place["noise"] + 1], 1.0)
        mean = jnp.sum(prior, 0, keepdims=True) / members
        anomaly = prior - mean
        spread = jnp.sum(anomaly * anomaly, 0, keepdims=True) * denominator
        total = spread + noise
        shrink = 1.0 / (1.0 + jnp.sqrt(noise / total))
        gain = ((value - mean) - shrink * anomaly) / total
        high = anomaly.astype(BF16).astype(F32)
        sides = jnp.concatenate([high, high, anomaly - high, jnp.zeros((16, CHUNK), F32)], 0)
        sides = sides.T.astype(BF16)
        gain_high, gain_low = halves(gain)
        gains = jnp.concatenate([gain_high, gain_low], 0)

        def column(name):
            return tall[:, place[name] : place[name] + 1]

        lev, lon, lat = places(column("site"), column("owner"))
        holder = jnp.where(lane.astype(F32) == column("owner"), 1.0, 0.0)
        weight = jnp.where(
            lane < INNER_ROW,
            jnp.sum(holder * links_of(b, col), 1, keepdims=True),
            jnp.where(
                lane < OUTER_ROW,
                jnp.sum(holder * links_of(b, inner_col), 1, keepdims=True),
                jnp.sum(holder * links_of(b, outer_col), 1, keepdims=True),
            ),
        )
        row_part = weight * denominator / (
            lev_square(row_lev.astype(F32), lev) * lon_square(row_lon.astype(F32), lon)
        )
        lat_part = 1.0 / lat_square(lane.astype(F32), lat)
        return sides, gains, row_part, lat_part, (lev, lon, lat, holder)

    def increment(x, sides, gains, local):
        weighted = dot(sides, centred_parts(x)) * local
        high, low = halves(weighted)
        first = dot(gains, high)
        return (first[:members] + first[members:]) + dot(gains[:members], low)

    def site_weights(where0, k1):
        lev0, lon0, lat0, holder = where0
        tall, wide = slots_of(1, k1)
        owner = wide[place["owner"] : place["owner"] + 1]
        lev, lon, lat = places(wide[place["site"] : place["site"] + 1], owner)
        pad = (-blocks) % 16
        spare = [jnp.zeros((pad, CAP), F32)] if pad else []
        table = jnp.concatenate(links[0] + spare, 0).astype(BF16)
        by_block = dot_lanes(holder.astype(BF16), table).astype(BF16)
        spare = [jnp.zeros((pad, CHUNK), F32)] if pad else []
        there = [jnp.where(owner == owners[j].astype(F32), 1.0, 0.0) for j in range(blocks)]
        weight = dot(by_block, jnp.concatenate(there + spare, 0).astype(BF16))
        square = lat_square(lat0, lat) * lon_square(lon0, lon) * lev_square(lev0, lev)
        return weight * denominator / square, wide

    direct = chunks == 1

    def analyse(b):
        if not direct:
            gained[...] = jnp.zeros_like(gained)

        def chunk(k):
            sides, gains, row_part, lat_part, where = batch_terms(b, k)
            if b == 0:

                def site_chunk(k1):
                    local, wide = site_weights(where, k1)
                    x = wide[:members]
                    moved = increment(x, sides, gains, local) * wide[members : members + 1]
                    for h in range(2):
                        at = EXT_ROWS + 2 * k1 + h
                        piece = slice(h * LATS, (h + 1) * LATS)
                        if direct:
                            fields[at] = x[:, piece] + moved[:, piece]
                        else:
                            before = jnp.where(k == 0, x[:, piece], fields[at])
                            fields[at] = before + moved[:, piece]

                for_each(chunks, site_chunk)
            for r in range(0, EXT_ROWS, 2):
                x = jnp.concatenate([fields[r], fields[r + 1]], 1)
                local = jnp.concatenate(
                    [lat_part * row_part[:, r : r + 1], lat_part * row_part[:, r + 1 : r + 2]], 1
                )
                moved = increment(x, sides, gains, local)
                moved = moved * jnp.concatenate([ocean[r], ocean[r + 1]], 1)
                for h in range(2):
                    piece = slice(h * LATS, (h + 1) * LATS)
                    if direct:
                        fields[r + h] = x[:, piece] + moved[:, piece]
                    else:
                        gained[r + h] = gained[r + h] + moved[:, piece]

        for_each(chunks, chunk)
        if not direct:
            for r in range(EXT_ROWS):
                fields[r] = fields[r] + gained[r]

    for b in range(BATCHES):
        analyse(b)

    lower = jnp.where(odd == 0, Y_ROW, CORE_ROW)
    upper = jnp.where(odd == 0, CORE_ROW, Y_ROW)
    east_row = jnp.where(even_col, INNER_ROW, OUTER_ROW)
    west_row = jnp.where(even_col, OUTER_ROW, INNER_ROW)
    for r in range(ROWS):
        lev, lon = r // LONS, r % LONS
        x = fields[r]
        lon_next = fields[r + 1] if lon < LONS - 1 else fields[east_row + lev]
        lon_prev = fields[r - 1] if lon > 0 else fields[west_row + lev]
        lat_next = jnp.where(lane < LATS - 1, pltpu.roll(x, LATS - 1, 1), 0.0)
        lat_prev = jnp.where(lane > 0, pltpu.roll(x, 1, 1), 0.0)
        vertical = fields[r ^ LONS] + fields[(lower if lev == 0 else upper) + lon]
        tendency = (
            -0.5 * zonal[r : r + 1, :] * (lon_next - lon_prev)
            + LATERAL_MIX * (lon_next + lon_prev + lat_next + lat_prev - 4.0 * x)
            + VERTICAL_MIX * (vertical - 2.0 * x)
        )
        out[pl.ds(r, members, stride=ROWS), :] = x + ocean[lon] * tendency


def swapped(x, axis, bit):
    return lax.ppermute(x, axis, [(i, i ^ bit) for i in range(lax.axis_size(axis))])


def shifted(x, axis, by):
    count = lax.axis_size(axis)
    return lax.ppermute(x, axis, [(i, (i + by) % count) for i in range(count)])


def local(state, observation_site, obs_count, measured_values, observation_noise, loc_pattern, ocean_mask, zonal_current):
    members = state.shape[0]
    columns = lax.axis_size("col")
    floors = lax.axis_size("gz")
    vmem = pl.BlockSpec(memory_space=pltpu.VMEM)
    smem = pl.BlockSpec(memory_space=pltpu.SMEM)
    height = members + 8
    level = members * LONS
    edge = members * LEVS + 8
    flat = state.reshape(members * ROWS, LATS)

    def like(*lengths):
        return [jax.ShapeDtypeStruct((length, LATS), F32) for length in lengths]

    kept, core_send, y_send, inner, outer = pl.pallas_call(
        functools.partial(pick_kernel, members, columns),
        out_shape=like(height, height + level, level, edge, edge),
        in_specs=[smem] * 2 + [vmem] * 5,
        out_specs=[vmem] * 5,
        name="pick_priors",
    )(obs_count, loc_pattern, observation_site, measured_values, observation_noise, ocean_mask, flat)

    core_edge = swapped(core_send, "gz", 1)
    mine = kept + core_edge[:height]
    ends = [(i, i + 1) for i in range(1, floors - 1, 2)]
    y_edge = lax.ppermute(y_send, "gz", ends + [(j, i) for i, j in ends])
    ring = [(i, (i + 1) % columns) for i in range(1, columns, 2)]
    outer = lax.ppermute(outer, "col", ring + [(j, i) for i, j in ring])
    bit = 2
    while bit < floors:
        mine = mine + swapped(mine, "gz", bit)
        bit *= 2
    if columns <= 2 * WINDOW + 1 and columns & (columns - 1) == 0:
        around = None
        inner = swapped(jnp.concatenate([mine, inner]), "col", 1)
        pair = jnp.stack([mine, inner[:height]])
        gathered = [pair] + [swapped(pair, "col", bit) for bit in range(2, columns, 2)]
    else:
        inner = swapped(inner, "col", 1)
        around = tuple(range(-WINDOW, WINDOW + 1)) if columns > 2 * WINDOW + 1 else tuple(range(columns))
        gathered = [(mine if by == 0 else shifted(mine, "col", -by))[None] for by in around]
    parts = tuple(part.shape[0] for part in gathered)
    other = [swapped(part, "gz", 1) for part in gathered]

    slots = min(sum(parts) * CAP, MEAN_COUNT * columns)
    chunks = -(-slots // CHUNK)
    rows = EXT_ROWS + 2 * chunks
    out = pl.pallas_call(
        functools.partial(step_kernel, members, parts, columns, around, chunks),
        out_shape=jax.ShapeDtypeStruct((members * ROWS, LATS), F32),
        in_specs=[vmem] * (7 + 2 * len(parts)),
        out_specs=vmem,
        scratch_shapes=[
            pltpu.VMEM((BATCHES, chunks * CHUNK + CAP, CAP), F32),
            pltpu.VMEM((rows, members, LATS), F32),
            pltpu.VMEM((EXT_ROWS if chunks > 1 else 1, members, LATS), F32),
        ],
        compiler_params=pltpu.CompilerParams(vmem_limit_bytes=48 * 1024 * 1024),
        name="analyse_and_step",
    )(
        ocean_mask, zonal_current.reshape(ROWS, LATS), flat, core_edge, y_edge, inner, outer, *gathered, *other
    )
    return out.reshape(state.shape)


def solution(mesh):
    in_specs = (
        P(None, "gz", "col", None),
        P(),
        P(None, "col"),
        P(None, "col"),
        P(None, "col"),
        P(None, None, "col"),
        P("col", None),
        P("gz", "col", None),
    )
    out_specs = P(None, "gz", "col", None)
    return jax.shard_map(local, mesh=mesh, in_specs=in_specs, out_specs=out_specs, check_vma=False)
```

```python
import functools

import jax
import jax.numpy as jnp
from jax import lax
from jax.experimental import pallas as pl
from jax.experimental.pallas import tpu as pltpu
from jax.sharding import PartitionSpec as P

LEVS = 2
LONS = 8
LATS = 128
BATCHES = 2
REACH = 3
CAP = 128
MEAN_COUNT = 32
WINDOW = 2 * REACH + 1
CHUNK = 256

CELLS = LEVS * LONS * LATS
ROWS = LEVS * LONS
CORE_ROW = 16
INNER_ROW = 24
Y_ROW = 26
OUTER_ROW = 34
EXT_ROWS = 36

LATERAL_MIX = 0.2
VERTICAL_MIX = 0.15

F32 = jnp.float32
BF16 = jnp.bfloat16


def iota(shape, dim):
    return lax.broadcasted_iota(jnp.int32, shape, dim)


def halves(x):
    high = x.astype(BF16)
    return high, (x - high.astype(F32)).astype(BF16)


def dot(a, b):
    return lax.dot_general(a, b, (((1,), (0,)), ((), ())), preferred_element_type=F32)


def dot_lanes(a, b):
    return lax.dot_general(a, b, (((1,), (1,)), ((), ())), preferred_element_type=F32)


def for_each(count, body):
    if count == 1:
        body(0)
    else:
        lax.fori_loop(0, count, lambda i, unused: (body(i), unused)[1], 0)


def rows_of(members):
    names = ("mask", "value", "noise", "links", "site", "occupied", "owner", "count")
    return {name: members + i for i, name in enumerate(names)}


def position():
    return lax.axis_index("col").astype(jnp.int32), lax.axis_index("gz").astype(jnp.int32)


def pick_kernel(members, columns, count, linked, site, value, noise, mask, state, kept, core_send, y_send, inner, outer):
    col, gz = position()
    core = gz % 2
    lane = iota((1, CAP), 1)
    at = pl.multiple_of(col * CAP, CAP)
    index, filled = [], []
    for b in range(BATCHES):
        occupied = lane < count[0, b]
        filled.append(occupied)
        index.append(jnp.where(occupied, site[b : b + 1, pl.ds(at, CAP)] - gz * CELLS, -1))
    wanted = jnp.concatenate(index, 1)
    total = jnp.zeros((3 * members + 16, BATCHES * CAP), F32)
    cell = iota((2 * LATS, BATCHES * CAP), 0)
    ocean = mask[...].astype(F32)
    for pair in range(ROWS // 2):
        left = []
        for r in (2 * pair, 2 * pair + 1):
            x = state[pl.ds(r, members, stride=ROWS), :]
            high = x.astype(BF16)
            rest = x - high.astype(F32)
            middle = rest.astype(BF16)
            low = (rest - middle.astype(F32)).astype(BF16)
            lon = r % LONS
            row = jnp.broadcast_to(ocean[lon : lon + 1, :], (16, LATS)).astype(BF16)
            left.append(jnp.concatenate([high, row, middle, low], 0))
        hit = jnp.where(cell + pair * 2 * LATS == wanted, 1.0, 0.0).astype(BF16)
        total = total + dot(jnp.concatenate(left, 1), hit)
    m = members
    height = m + 8
    picked = (total[:m] + total[m + 16 : 2 * m + 16]) + total[2 * m + 16 :]
    first = jnp.where(gz == 0, 1.0, 0.0)
    for b in range(BATCHES):
        here = slice(b * CAP, (b + 1) * CAP)
        once = jnp.where(filled[b], first, 0.0)
        links = jnp.concatenate([linked[b].astype(F32), jnp.zeros((1, CAP - columns), F32)], 1)
        tail = [
            total[m : m + 1, here],
            value[b : b + 1, :] * once,
            noise[b : b + 1, :] * once,
            links * first,
            site[b : b + 1, pl.ds(at, CAP)].astype(F32) * once,
            once,
            once * col.astype(F32),
            jnp.full((1, CAP), count[0, b].astype(F32) * first),
        ]
        block = jnp.concatenate([picked[:, here]] + tail, 0)

        @pl.when(core == b)
        def _():
            kept[...] = block

        @pl.when(core != b)
        def _():
            core_send[:height, :] = block

    for member in range(members):
        up = state[pl.ds(pl.multiple_of(member * ROWS + (1 - core) * LONS, LONS), LONS), :]
        core_send[height + member * LONS : height + (member + 1) * LONS, :] = up
        down = state[pl.ds(pl.multiple_of(member * ROWS + core * LONS, LONS), LONS), :]
        y_send[member * LONS : (member + 1) * LONS, :] = down
    even = col % 2 == 0
    for lev in range(LEVS):
        west = state[pl.ds(lev * LONS, members, stride=ROWS), :]
        east = state[pl.ds(lev * LONS + LONS - 1, members, stride=ROWS), :]
        inner[lev * members : (lev + 1) * members, :] = jnp.where(even, east, west)
        outer[lev * members : (lev + 1) * members, :] = jnp.where(even, west, east)
    west = jnp.broadcast_to(ocean[:1], (8, LATS))
    east = jnp.broadcast_to(ocean[LONS - 1 :], (8, LATS))
    inner[LEVS * members :, :] = jnp.where(even, east, west)
    outer[LEVS * members :, :] = jnp.where(even, west, east)


def place_terms(col, gz, columns):
    lon_all = columns * LONS
    odd = gz % 2
    even_col = col % 2 == 0
    lane = iota((1, LATS), 1)
    above, below = LEVS * gz + LEVS, LEVS * gz - 1
    own = lane < ROWS
    near = (lane >= CORE_ROW) & (lane < INNER_ROW)
    far = (lane >= Y_ROW) & (lane < OUTER_ROW)
    row_lev = LEVS * gz + jnp.where(own, lane // LONS, lane % LEVS)
    row_lev = jnp.where(near, jnp.where(odd == 0, above, below), row_lev)
    row_lev = jnp.where(far, jnp.where(odd == 0, below, above), row_lev)
    west_lon = (col * LONS + lon_all - 1) % lon_all
    east_lon = (col * LONS + LONS) % lon_all
    inner = (lane >= INNER_ROW) & (lane < Y_ROW)
    row_lon = col * LONS + jnp.where(far, lane - Y_ROW, lane % LONS)
    row_lon = jnp.where(inner, jnp.where(even_col, east_lon, west_lon), row_lon)
    row_lon = jnp.where(lane >= OUTER_ROW, jnp.where(even_col, west_lon, east_lon), row_lon)
    west_col = (col + columns - 1) % columns
    east_col = (col + 1) % columns
    inner_col = jnp.where(even_col, east_col, west_col)
    outer_col = jnp.where(even_col, west_col, east_col)
    return row_lev.astype(F32), row_lon.astype(F32), inner, inner_col, outer_col


def centred_parts(x):
    x = x - jnp.sum(x, 0, keepdims=True) * (1.0 / x.shape[0])
    high, low = halves(x)
    return jnp.concatenate([high, low, high, jnp.zeros((16, x.shape[1]), BF16)], 0)


def increment(x, sides, gains, local):
    members = x.shape[0]
    weighted = dot(sides, centred_parts(x)) * local
    high, low = halves(weighted)
    first = dot(gains, high)
    return (first[:members] + first[members:]) + dot(gains[:members], low)


def move_rows(fields, gained, first, last, ocean, terms, b, chunks):
    sides, gains, row_part, lat_part = terms

    def chunk(k):
        t = b * chunks + k
        for r in range(first, last, 2):
            at = r - first
            x = jnp.concatenate([fields[at], fields[at + 1]], 1)
            tapers = [lat_part[t] * row_part[t, :, r + h : r + h + 1] for h in range(2)]
            moved = increment(x, sides[t], gains[t], jnp.concatenate(tapers, 1))
            moved = moved * jnp.concatenate([ocean[at], ocean[at + 1]], 1)
            for h in range(2):
                piece = slice(h * LATS, (h + 1) * LATS)
                if chunks == 1:
                    fields[at + h] = x[:, piece] + moved[:, piece]
                else:
                    gained[at + h] = gained[at + h] + moved[:, piece]

    if chunks > 1:
        gained[...] = jnp.zeros_like(gained)
    for_each(chunks, chunk)
    if chunks > 1:
        for at in range(last - first):
            fields[at] = fields[at] + gained[at]


def near_kernel(members, parts, columns, around, chunks, mask, state, core_edge, inner, *rest):
    mine_parts, other_parts = rest[: len(parts)], rest[len(parts) : 2 * len(parts)]
    fields, sides, gains, row_terms, lat_terms, packed, gained = rest[2 * len(parts) :]
    mine = [part.at[i] for part, size in zip(mine_parts, parts) for i in range(size)]
    other = [part.at[i] for part, size in zip(other_parts, parts) for i in range(size)]
    blocks = len(mine)
    col, gz = position()
    core = gz % 2
    lon_all = columns * LONS
    place = rows_of(members)
    denominator = 1.0 / (members - 1)
    height = members + 8
    owners = [col ^ j if around is None else (col + around[j] + columns) % columns for j in range(blocks)]

    links = []
    packed[...] = jnp.zeros_like(packed)
    for b in range(BATCHES):
        start = 0
        own_links = []
        for j in range(blocks):
            block = jnp.where(core == b, mine[j][...], other[j][...])
            own_links.append(block[place["links"] : place["links"] + 1, :])
            tall = jnp.concatenate([block, jnp.zeros((LATS - height, CAP), F32)], 0)
            packed[b, pl.ds(start, CAP), :] = tall.T
            start = start + block[place["count"], 0].astype(jnp.int32)
        links.append(own_links)

    inner_start = inner.shape[0] - (members * LEVS + 8)
    for r in range(ROWS):
        fields[r] = state[pl.ds(r, members, stride=ROWS), :]
    for lon in range(LONS):
        fields[CORE_ROW + lon] = core_edge[pl.ds(height + lon, members, stride=LONS), :]
    for lev in range(LEVS):
        at = inner_start + lev * members
        fields[INNER_ROW + lev] = inner[at : at + members, :]
    wet = mask[...].astype(F32)
    ocean = [wet[lon : lon + 1] for lon in range(LONS)] * 3
    at = inner_start + members * LEVS
    ocean += [inner[at : at + 1, :]] * LEVS

    lane = iota((1, LATS), 1)
    row_lev, row_lon, inside, inner_col, outer_col = place_terms(col, gz, columns)

    def links_of(b, target):
        row = jnp.zeros((1, CAP), F32)
        for j in range(blocks):
            row = row + jnp.where(owners[j] == target, links[b][j], 0.0)
        return row

    def places(site, owner):
        site = site.astype(jnp.int32)
        lev = site // (LONS * LATS)
        lon = owner.astype(jnp.int32) * LONS + site // LATS % LONS
        return lev.astype(F32), lon.astype(F32), (site % LATS).astype(F32)

    def lon_square(a, b):
        gap = jnp.abs(a - b)
        gap = jnp.minimum(gap, lon_all - gap) * (1.0 / (2.0 * LONS))
        return 1.0 + gap * gap

    def lev_square(a, b):
        gap = (a - b) * 0.5
        return 1.0 + gap * gap

    def lat_square(a, b):
        gap = (a - b) * (1.0 / (LATS // 8))
        return 1.0 + gap * gap

    def slots_of(b, k):
        start = k * CHUNK if isinstance(k, int) else pl.multiple_of(k * CHUNK, CHUNK)
        tall = packed[b, pl.ds(start, CHUNK), :]
        return tall, tall.T

    def batch_terms(b, k):
        tall, wide = slots_of(b, k)
        occupied = wide[place["occupied"] : place["occupied"] + 1]
        if b == 0:
            prior = wide[:members]
        else:
            prior = jnp.concatenate([fields[Y_ROW + 2 * k], fields[Y_ROW + 2 * k + 1]], 1) * occupied
        value = wide[place["value"] : place["value"] + 1]
        noise = jnp.where(occupied > 0, wide[place["noise"] : place["noise"] + 1], 1.0)
        mean = jnp.sum(prior, 0, keepdims=True) / members
        anomaly = prior - mean
        spread = jnp.sum(anomaly * anomaly, 0, keepdims=True) * denominator
        total = spread + noise
        shrink = 1.0 / (1.0 + jnp.sqrt(noise / total))
        gain = ((value - mean) - shrink * anomaly) / total
        high = anomaly.astype(BF16).astype(F32)
        stack = jnp.concatenate([high, high, anomaly - high, jnp.zeros((16, CHUNK), F32)], 0)
        t = b * chunks + k
        sides[t] = stack.T.astype(BF16)
        gains[t] = jnp.concatenate(halves(gain), 0)

        def column(name):
            return tall[:, place[name] : place[name] + 1]

        lev, lon, lat = places(column("site"), column("owner"))
        holder = jnp.where(lane.astype(F32) == column("owner"), 1.0, 0.0)
        weight = [jnp.sum(holder * links_of(b, c), 1, keepdims=True) for c in (col, inner_col, outer_col)]
        weight = jnp.where(inside, weight[1], jnp.where(lane < OUTER_ROW, weight[0], weight[2]))
        row_terms[t] = weight * denominator / (lev_square(row_lev, lev) * lon_square(row_lon, lon))
        lat_terms[t] = 1.0 / lat_square(lane.astype(F32), lat)
        return lev, lon, lat, holder

    def site_weights(where0, k1):
        lev0, lon0, lat0, holder = where0
        tall, wide = slots_of(1, k1)
        owner = wide[place["owner"] : place["owner"] + 1]
        lev, lon, lat = places(wide[place["site"] : place["site"] + 1], owner)
        pad = (-blocks) % 16
        spare = [jnp.zeros((pad, CAP), F32)] if pad else []
        table = jnp.concatenate(links[0] + spare, 0).astype(BF16)
        by_block = dot_lanes(holder.astype(BF16), table).astype(BF16)
        spare = [jnp.zeros((pad, CHUNK), F32)] if pad else []
        there = [jnp.where(owner == owners[j].astype(F32), 1.0, 0.0) for j in range(blocks)]
        weight = dot(by_block, jnp.concatenate(there + spare, 0).astype(BF16))
        square = lat_square(lat0, lat) * lon_square(lon0, lon) * lev_square(lev0, lev)
        return weight * denominator / square, wide

    def first_terms(k):
        where = batch_terms(0, k)

        def site_chunk(k1):
            taper, wide = site_weights(where, k1)
            x = wide[:members]
            moved = increment(x, sides[k], gains[k], taper) * wide[members : members + 1]
            for h in range(2):
                at = Y_ROW + 2 * k1 + h
                piece = slice(h * LATS, (h + 1) * LATS)
                before = x[:, piece] if chunks == 1 else jnp.where(k == 0, x[:, piece], fields[at])
                fields[at] = before + moved[:, piece]

        for_each(chunks, site_chunk)

    terms = (sides, gains, row_terms, lat_terms)
    for_each(chunks, first_terms)
    for_each(chunks, lambda k: (batch_terms(1, k), None)[1])
    for b in range(BATCHES):
        move_rows(fields, gained, 0, Y_ROW, ocean, terms, b, chunks)


def far_kernel(
    members, columns, floors, chunks, mask, zonal, near, y_edge, outer, sides, gains, row_terms, lat_terms, out, fields, gained
):
    col, gz = position()
    core = gz % 2
    even_col = col % 2 == 0
    lane = iota((1, LATS), 1)
    outer_at = OUTER_ROW - Y_ROW
    beyond = gz + 2 * core - 1
    inside = jnp.where((beyond >= 0) & (beyond < floors), 1.0, 0.0)
    for lon in range(LONS):
        fields[lon] = y_edge[pl.ds(lon, members, stride=LONS), :] * inside
    for lev in range(LEVS):
        fields[outer_at + lev] = outer[lev * members : (lev + 1) * members, :]
    wet = mask[...].astype(F32)
    ocean = [wet[lon : lon + 1] for lon in range(LONS)]
    edge = members * LEVS
    terms = (sides, gains, row_terms, lat_terms)
    for b in range(BATCHES):
        move_rows(fields, gained, Y_ROW, EXT_ROWS, ocean + [outer[edge : edge + 1, :]] * LEVS, terms, b, chunks)

    for r in range(ROWS):
        lev, lon = r // LONS, r % LONS
        x = near[r]
        side = [near[INNER_ROW + lev], fields[outer_at + lev]]
        lon_next = near[r + 1] if lon < LONS - 1 else jnp.where(even_col, side[0], side[1])
        lon_prev = near[r - 1] if lon > 0 else jnp.where(even_col, side[1], side[0])
        lat_next = jnp.where(lane < LATS - 1, pltpu.roll(x, LATS - 1, 1), 0.0)
        lat_prev = jnp.where(lane > 0, pltpu.roll(x, 1, 1), 0.0)
        over = jnp.where(core == 1 - lev, near[CORE_ROW + lon], fields[lon])
        vertical = near[r ^ LONS] + over
        tendency = (
            -0.5 * zonal[r : r + 1, :] * (lon_next - lon_prev)
            + LATERAL_MIX * (lon_next + lon_prev + lat_next + lat_prev - 4.0 * x)
            + VERTICAL_MIX * (vertical - 2.0 * x)
        )
        out[pl.ds(r, members, stride=ROWS), :] = x + ocean[lon] * tendency


def room(mebibytes):
    return pltpu.CompilerParams(vmem_limit_bytes=mebibytes * 1024 * 1024)


def swapped(x, axis, bit):
    return lax.ppermute(x, axis, [(i, i ^ bit) for i in range(lax.axis_size(axis))])


def shifted(x, axis, by):
    count = lax.axis_size(axis)
    return lax.ppermute(x, axis, [(i, (i + by) % count) for i in range(count)])


def local(state, observation_site, obs_count, measured_values, observation_noise, loc_pattern, ocean_mask, zonal_current):
    members = state.shape[0]
    columns = lax.axis_size("col")
    floors = lax.axis_size("gz")
    vmem = pl.BlockSpec(memory_space=pltpu.VMEM)
    smem = pl.BlockSpec(memory_space=pltpu.SMEM)
    height = members + 8
    level = members * LONS
    edge = members * LEVS + 8
    flat = state.reshape(members * ROWS, LATS)

    def like(*lengths):
        return [pltpu.VMEM((length, LATS), F32) for length in lengths]

    kept, core_send, y_send, inner, outer = pl.pallas_call(
        functools.partial(pick_kernel, members, columns),
        out_shape=like(height, height + level, level, edge, edge),
        in_specs=[smem] + [vmem] * 6,
        out_specs=[vmem] * 5,
        name="pick_priors",
    )(
        obs_count.reshape(1, BATCHES),
        loc_pattern.reshape(BATCHES, 1, columns),
        observation_site,
        measured_values,
        observation_noise,
        ocean_mask,
        flat,
    )

    core_edge = swapped(core_send, "gz", 1)
    mine = kept + core_edge[:height]
    for bit in range(2, floors, 2):
        mine = mine + swapped(mine, "gz", bit)
    if columns <= 2 * WINDOW + 1 and columns & (columns - 1) == 0:
        around = None
        inner = swapped(jnp.concatenate([mine, inner]), "col", 1)
        pair = jnp.stack([mine, inner[:height]])
        gathered = [pair] + [swapped(pair, "col", bit) for bit in range(2, columns, 2)]
    else:
        inner = swapped(inner, "col", 1)
        around = tuple(range(-WINDOW, WINDOW + 1)) if columns > 2 * WINDOW + 1 else tuple(range(columns))
        gathered = [(mine if by == 0 else shifted(mine, "col", -by))[None] for by in around]

    ends = [(i, i + 1) for i in range(1, floors - 1, 2)]
    ends += [(j, i) for i, j in ends]
    ends += [(i, i) for i in range(floors) if i not in dict(ends)]
    y_edge = lax.ppermute(y_send, "gz", ends)
    ring = [(i, (i + 1) % columns) for i in range(1, columns, 2)]
    outer = lax.ppermute(outer, "col", ring + [(j, i) for i, j in ring])

    parts = tuple(part.shape[0] for part in gathered)
    other = [swapped(part, "gz", 1) for part in gathered]

    slots = min(sum(parts) * CAP, MEAN_COUNT * columns)
    chunks = -(-slots // CHUNK)
    rows = Y_ROW + 2 * chunks
    several = chunks > 1
    count = BATCHES * chunks
    limit = room(48 if several else 16)
    near, *terms = pl.pallas_call(
        functools.partial(near_kernel, members, parts, columns, around, chunks),
        out_shape=[
            pltpu.VMEM((rows, members, LATS), F32),
            pltpu.VMEM((count, CHUNK, CHUNK), BF16),
            pltpu.VMEM((count, 2 * members, CHUNK), BF16),
            pltpu.VMEM((count, CHUNK, LATS), F32),
            pltpu.VMEM((count, CHUNK, LATS), F32),
        ],
        in_specs=[vmem] * (4 + 2 * len(parts)),
        out_specs=[vmem] * 5,
        scratch_shapes=[
            pltpu.VMEM((BATCHES, chunks * CHUNK + CAP, CAP), F32),
            pltpu.VMEM((Y_ROW if several else 1, members, LATS), F32),
        ],
        compiler_params=limit,
        cost_estimate=pl.CostEstimate(flops=0, bytes_accessed=0, transcendentals=0),
        name="analyse_near",
    )(ocean_mask, flat, core_edge, inner, *gathered, *other)
    out = pl.pallas_call(
        functools.partial(far_kernel, members, columns, floors, chunks),
        out_shape=jax.ShapeDtypeStruct((members * ROWS, LATS), F32),
        in_specs=[vmem] * 9,
        out_specs=vmem,
        scratch_shapes=[
            pltpu.VMEM((EXT_ROWS - Y_ROW, members, LATS), F32),
            pltpu.VMEM((EXT_ROWS - Y_ROW if several else 1, members, LATS), F32),
        ],
        compiler_params=limit,
        name="analyse_far_and_step",
    )(ocean_mask, zonal_current.reshape(ROWS, LATS), near, y_edge, outer, *terms)
    return out.reshape(state.shape)


def solution(mesh):
    in_specs = (
        P(None, "gz", "col", None),
        P(),
        P(None, "col"),
        P(None, "col"),
        P(None, "col"),
        P(None, None, "col"),
        P("col", None),
        P("gz", "col", None),
    )
    out_specs = P(None, "gz", "col", None)
    return jax.shard_map(local, mesh=mesh, in_specs=in_specs, out_specs=out_specs, check_vma=False)
```

```python
import functools

import jax
import jax.numpy as jnp
from jax import lax
from jax.experimental import pallas as pl
from jax.experimental.pallas import tpu as pltpu
from jax.sharding import PartitionSpec as P

LEVS = 2
LONS = 8
LATS = 128
BATCHES = 2
REACH = 3
CAP = 128
MEAN_COUNT = 32
WINDOW = 2 * REACH + 1
CHUNK = 256

CELLS = LEVS * LONS * LATS
ROWS = LEVS * LONS
CORE_ROW = 16
INNER_ROW = 24
Y_ROW = 26
OUTER_ROW = 34
EXT_ROWS = 36
ROW_LIMIT = 40
ROW_COLUMN = 24

LATERAL_MIX = 0.2
VERTICAL_MIX = 0.15

F32 = jnp.float32
BF16 = jnp.bfloat16


def iota(shape, dim):
    return lax.broadcasted_iota(jnp.int32, shape, dim)


def halves(x):
    high = x.astype(BF16)
    return high, (x - high.astype(F32)).astype(BF16)


def dot(a, b):
    return lax.dot_general(a, b, (((1,), (0,)), ((), ())), preferred_element_type=F32)


def dot_lanes(a, b):
    return lax.dot_general(a, b, (((1,), (1,)), ((), ())), preferred_element_type=F32)


def for_each(count, body):
    if count == 1:
        body(0)
    else:
        lax.fori_loop(0, count, lambda i, unused: (body(i), unused)[1], 0)


def rows_of(members):
    names = ("mask", "value", "noise", "links", "site", "occupied", "owner", "count")
    return {name: members + i for i, name in enumerate(names)}


def position():
    return lax.axis_index("col").astype(jnp.int32), lax.axis_index("gz").astype(jnp.int32)


def pick_kernel(members, columns, count, linked, site, value, noise, mask, state, kept, core_send, y_send, inner, outer, rows):
    col, gz = position()
    core = gz % 2
    lane = iota((1, CAP), 1)
    at = pl.multiple_of(col * CAP, CAP)
    index, filled = [], []
    for b in range(BATCHES):
        occupied = lane < count[0, b]
        filled.append(occupied)
        index.append(jnp.where(occupied, site[b : b + 1, pl.ds(at, CAP)] - gz * CELLS, -1))
    wanted = jnp.concatenate(index, 1)
    total = jnp.zeros((3 * members + 16, BATCHES * CAP), F32)
    cell = iota((2 * LATS, BATCHES * CAP), 0)
    ocean = mask[...].astype(F32)
    for pair in range(ROWS // 2):
        left = []
        for r in (2 * pair, 2 * pair + 1):
            x = state[pl.ds(r, members, stride=ROWS), :]
            rows[r] = x
            high = x.astype(BF16)
            rest = x - high.astype(F32)
            middle = rest.astype(BF16)
            low = (rest - middle.astype(F32)).astype(BF16)
            lon = r % LONS
            row = jnp.broadcast_to(ocean[lon : lon + 1, :], (16, LATS)).astype(BF16)
            left.append(jnp.concatenate([high, row, middle, low], 0))
        hit = jnp.where(cell + pair * 2 * LATS == wanted, 1.0, 0.0).astype(BF16)
        total = total + dot(jnp.concatenate(left, 1), hit)
    m = members
    height = m + 8
    picked = (total[:m] + total[m + 16 : 2 * m + 16]) + total[2 * m + 16 :]
    first = jnp.where(gz == 0, 1.0, 0.0)
    for b in range(BATCHES):
        here = slice(b * CAP, (b + 1) * CAP)
        once = jnp.where(filled[b], first, 0.0)
        links = jnp.concatenate([linked[b].astype(F32), jnp.zeros((1, CAP - columns), F32)], 1)
        tail = [
            total[m : m + 1, here],
            value[b : b + 1, :] * once,
            noise[b : b + 1, :] * once,
            links * first,
            site[b : b + 1, pl.ds(at, CAP)].astype(F32) * once,
            once,
            once * col.astype(F32),
            jnp.full((1, CAP), count[0, b].astype(F32) * first),
        ]
        block = jnp.concatenate([picked[:, here]] + tail, 0)

        @pl.when(core == b)
        def _():
            kept[...] = block

        @pl.when(core != b)
        def _():
            core_send[:height, :] = block

    for member in range(members):
        up = state[pl.ds(pl.multiple_of(member * ROWS + (1 - core) * LONS, LONS), LONS), :]
        core_send[height + member * LONS : height + (member + 1) * LONS, :] = up
        down = state[pl.ds(pl.multiple_of(member * ROWS + core * LONS, LONS), LONS), :]
        y_send[member * LONS : (member + 1) * LONS, :] = down
    even = col % 2 == 0
    for lev in range(LEVS):
        west = state[pl.ds(lev * LONS, members, stride=ROWS), :]
        east = state[pl.ds(lev * LONS + LONS - 1, members, stride=ROWS), :]
        inner[lev * members : (lev + 1) * members, :] = jnp.where(even, east, west)
        outer[lev * members : (lev + 1) * members, :] = jnp.where(even, west, east)
    west = jnp.broadcast_to(ocean[:1], (8, LATS))
    east = jnp.broadcast_to(ocean[LONS - 1 :], (8, LATS))
    inner[LEVS * members :, :] = jnp.where(even, east, west)
    outer[LEVS * members :, :] = jnp.where(even, west, east)


def place_terms(col, gz, columns):
    lon_all = columns * LONS
    odd = gz % 2
    even_col = col % 2 == 0
    at = iota((ROW_LIMIT, 1), 0)
    above, below = LEVS * gz + LEVS, LEVS * gz - 1
    own = at < ROWS
    near = (at >= CORE_ROW) & (at < INNER_ROW)
    far = (at >= Y_ROW) & (at < OUTER_ROW)
    row_lev = LEVS * gz + jnp.where(own, at // LONS, at % LEVS)
    row_lev = jnp.where(near, jnp.where(odd == 0, above, below), row_lev)
    row_lev = jnp.where(far, jnp.where(odd == 0, below, above), row_lev)
    west_lon = (col * LONS + lon_all - 1) % lon_all
    east_lon = (col * LONS + LONS) % lon_all
    inner = (at >= INNER_ROW) & (at < Y_ROW)
    row_lon = col * LONS + jnp.where(far, at - Y_ROW, at % LONS)
    row_lon = jnp.where(inner, jnp.where(even_col, east_lon, west_lon), row_lon)
    row_lon = jnp.where(at >= OUTER_ROW, jnp.where(even_col, west_lon, east_lon), row_lon)
    west_col = (col + columns - 1) % columns
    east_col = (col + 1) % columns
    inner_col = jnp.where(even_col, east_col, west_col)
    outer_col = jnp.where(even_col, west_col, east_col)
    return row_lev.astype(F32), row_lon.astype(F32), inner, at >= OUTER_ROW, inner_col, outer_col


def centred_parts(x):
    x = x - jnp.sum(x, 0, keepdims=True) * (1.0 / x.shape[0])
    high, low = halves(x)
    return jnp.concatenate([high, low, high, jnp.zeros((16, x.shape[1]), BF16)], 0)


def increment(x, sides, gains, local):
    members = x.shape[0]
    weighted = dot(sides, centred_parts(x)) * local
    high, low = halves(weighted)
    first = dot(gains, high)
    return (first[:members] + first[members:]) + dot(gains[:members], low)


def move_rows(fields, gained, first, last, ocean, terms, b, chunks):
    sides, gains, row_part, lat_part = terms

    def chunk(k):
        t = b * chunks + k
        for r in range(first, last, 2):
            at = r - first
            x = jnp.concatenate([fields[at], fields[at + 1]], 1)
            columns = [ROW_COLUMN + r + h for h in range(2)]
            tapers = [lat_part[t] * row_part[t, :, c : c + 1] for c in columns]
            moved = increment(x, sides[t], gains[t], jnp.concatenate(tapers, 1))
            moved = moved * jnp.concatenate([ocean[at], ocean[at + 1]], 1)
            for h in range(2):
                piece = slice(h * LATS, (h + 1) * LATS)
                if chunks == 1:
                    fields[at + h] = x[:, piece] + moved[:, piece]
                else:
                    gained[at + h] = gained[at + h] + moved[:, piece]

    if chunks > 1:
        gained[...] = jnp.zeros_like(gained)
    for_each(chunks, chunk)
    if chunks > 1:
        for at in range(last - first):
            fields[at] = fields[at] + gained[at]


def near_kernel(members, parts, columns, around, chunks, mask, own, core_edge, inner, *rest):
    mine_parts, other_parts = rest[: len(parts)], rest[len(parts) : 2 * len(parts)]
    fields, sides, gains, row_terms, lat_terms, packed, gained = rest[2 * len(parts) :]
    mine = [part.at[i] for part, size in zip(mine_parts, parts) for i in range(size)]
    other = [part.at[i] for part, size in zip(other_parts, parts) for i in range(size)]
    blocks = len(mine)
    col, gz = position()
    core = gz % 2
    lon_all = columns * LONS
    place = rows_of(members)
    denominator = 1.0 / (members - 1)
    height = members + 8
    owners = [col ^ j if around is None else (col + around[j] + columns) % columns for j in range(blocks)]

    lane = iota((1, LATS), 1)
    pad = (-blocks) % 16
    tables = []
    for b in range(BATCHES):
        start = jnp.zeros((1, CAP), jnp.int32)
        tiles = [jnp.zeros((height, CAP), F32)] * (chunks * CHUNK // CAP)
        links = []
        for j in range(blocks):
            block = jnp.where(core == b, mine[j][...], other[j][...])
            links.append(block[place["links"] : place["links"] + 1, :])
            if j == 0:
                tiles[0] = block
            else:
                shift = start % CAP
                turned = pltpu.roll(block, shift[0, 0], 1)
                into = start // CAP + jnp.where(lane < shift, 1, 0)
                tiles = [tile + jnp.where(into == i, turned, 0.0) for i, tile in enumerate(tiles)]
            start = start + block[place["count"] : place["count"] + 1, :].astype(jnp.int32)
        for i, tile in enumerate(tiles):
            packed[b, i] = tile
        tables.append(jnp.concatenate(links + [jnp.zeros((pad, CAP), F32)] * (pad > 0), 0).astype(BF16))

    inner_start = inner.shape[0] - (members * LEVS + 8)
    for r in range(ROWS):
        fields[r] = own[r]
    for lon in range(LONS):
        fields[CORE_ROW + lon] = core_edge[pl.ds(height + lon, members, stride=LONS), :]
    for lev in range(LEVS):
        at = inner_start + lev * members
        fields[INNER_ROW + lev] = inner[at : at + members, :]
    wet = mask[...].astype(F32)
    ocean = [wet[lon : lon + 1] for lon in range(LONS)] * 3
    at = inner_start + members * LEVS
    ocean += [inner[at : at + 1, :]] * LEVS

    row_lev, row_lon, inside, outside, inner_col, outer_col = place_terms(col, gz, columns)

    def places(site, owner):
        site = site.astype(jnp.int32)
        lev = site // (LONS * LATS)
        lon = owner.astype(jnp.int32) * LONS + site // LATS % LONS
        return lev.astype(F32), lon.astype(F32), (site % LATS).astype(F32)

    def lon_square(a, b):
        gap = jnp.abs(a - b)
        gap = jnp.minimum(gap, lon_all - gap) * (1.0 / (2.0 * LONS))
        return 1.0 + gap * gap

    def lev_square(a, b):
        gap = (a - b) * 0.5
        return 1.0 + gap * gap

    def lat_square(a, b):
        gap = (a - b) * (1.0 / (LATS // 8))
        return 1.0 + gap * gap

    def slots_of(b, k):
        wide = jnp.concatenate([packed[b, 2 * k], packed[b, 2 * k + 1]], 1)

        def row(name):
            return wide[place[name] : place[name] + 1]

        return wide, row

    def batch_terms(b, k):
        wide, row = slots_of(b, k)
        occupied = row("occupied")
        if b == 0:
            prior = wide[:members]
        else:
            prior = jnp.concatenate([fields[Y_ROW + 2 * k], fields[Y_ROW + 2 * k + 1]], 1) * occupied
        noise = jnp.where(occupied > 0, row("noise"), 1.0)
        mean = jnp.sum(prior, 0, keepdims=True) / members
        anomaly = prior - mean
        spread = jnp.sum(anomaly * anomaly, 0, keepdims=True) * denominator
        total = spread + noise
        shrink = 1.0 / (1.0 + jnp.sqrt(noise / total))
        gain = ((row("value") - mean) - shrink * anomaly) / total
        high = anomaly.astype(BF16).astype(F32)
        stack = jnp.concatenate([high, high, anomaly - high, jnp.zeros((16, CHUNK), F32)], 0)
        t = b * chunks + k
        sides[t] = stack.T.astype(BF16)
        gains[t] = jnp.concatenate(halves(gain), 0)

    def batch_tapers(b, k):
        wide, row = slots_of(b, k)
        owner = row("owner")
        lev, lon, lat = places(row("site"), owner)
        holder = jnp.where(iota((CAP, CHUNK), 0).astype(F32) == owner, 1.0, 0.0).astype(BF16)
        by_block = dot(tables[b], holder)
        weight = []
        for target in (col, inner_col, outer_col):
            total = jnp.zeros((1, CHUNK), F32)
            for j in range(blocks):
                total = total + jnp.where(owners[j] == target, by_block[j : j + 1], 0.0)
            weight.append(total)
        weight = jnp.where(inside, weight[1], jnp.where(outside, weight[2], weight[0]))
        weight = weight * denominator / (lev_square(row_lev, lev) * lon_square(row_lon, lon))
        spare = LATS - ROW_COLUMN - ROW_LIMIT
        table = jnp.concatenate(
            [lat, lev, lon, jnp.zeros((5, CHUNK), F32), by_block[:16], weight, jnp.zeros((spare, CHUNK), F32)], 0
        )
        t = b * chunks + k
        row_terms[t] = table.T
        lat_terms[t] = 1.0 / lat_square(lane.astype(F32), row_terms[t, :, 0:1])

    def site_weights(k0, k1):
        wide, row = slots_of(1, k1)
        owner = row("owner")
        lev, lon, lat = places(row("site"), owner)
        there = [jnp.where(owner == owners[j].astype(F32), 1.0, 0.0) for j in range(blocks)]
        there += [jnp.zeros((pad, CHUNK), F32)] * (pad > 0)
        weight = dot(row_terms[k0, :, 8:24].astype(BF16), jnp.concatenate(there, 0).astype(BF16))
        lat0, lev0, lon0 = [row_terms[k0, :, i : i + 1] for i in range(3)]
        square = lat_square(lat0, lat) * lon_square(lon0, lon) * lev_square(lev0, lev)
        return weight * denominator / square, wide

    def first_terms(k):
        batch_terms(0, k)
        batch_tapers(0, k)

        def site_chunk(k1):
            taper, wide = site_weights(k, k1)
            x = wide[:members]
            moved = increment(x, sides[k], gains[k], taper) * wide[members : members + 1]
            for h in range(2):
                at = Y_ROW + 2 * k1 + h
                piece = slice(h * LATS, (h + 1) * LATS)
                before = x[:, piece] if chunks == 1 else jnp.where(k == 0, x[:, piece], fields[at])
                fields[at] = before + moved[:, piece]

        for_each(chunks, site_chunk)

    def second_terms(k):
        batch_terms(1, k)
        batch_tapers(1, k)

    terms = (sides, gains, row_terms, lat_terms)
    for_each(chunks, first_terms)
    for_each(chunks, second_terms)
    for b in range(BATCHES):
        move_rows(fields, gained, 0, Y_ROW, ocean, terms, b, chunks)


def far_kernel(
    members, columns, floors, chunks, mask, zonal, near, y_edge, outer, sides, gains, row_terms, lat_terms, out, fields, gained
):
    col, gz = position()
    core = gz % 2
    even_col = col % 2 == 0
    lane = iota((1, LATS), 1)
    outer_at = OUTER_ROW - Y_ROW
    beyond = gz + 2 * core - 1
    inside = jnp.where((beyond >= 0) & (beyond < floors), 1.0, 0.0)
    for lon in range(LONS):
        fields[lon] = y_edge[pl.ds(lon, members, stride=LONS), :] * inside
    for lev in range(LEVS):
        fields[outer_at + lev] = outer[lev * members : (lev + 1) * members, :]
    wet = mask[...].astype(F32)
    ocean = [wet[lon : lon + 1] for lon in range(LONS)]
    edge = members * LEVS
    terms = (sides, gains, row_terms, lat_terms)
    for b in range(BATCHES):
        move_rows(fields, gained, Y_ROW, EXT_ROWS, ocean + [outer[edge : edge + 1, :]] * LEVS, terms, b, chunks)

    for r in range(ROWS):
        lev, lon = r // LONS, r % LONS
        x = near[r]
        side = [near[INNER_ROW + lev], fields[outer_at + lev]]
        lon_next = near[r + 1] if lon < LONS - 1 else jnp.where(even_col, side[0], side[1])
        lon_prev = near[r - 1] if lon > 0 else jnp.where(even_col, side[1], side[0])
        lat_next = jnp.where(lane < LATS - 1, pltpu.roll(x, LATS - 1, 1), 0.0)
        lat_prev = jnp.where(lane > 0, pltpu.roll(x, 1, 1), 0.0)
        over = jnp.where(core == 1 - lev, near[CORE_ROW + lon], fields[lon])
        vertical = near[r ^ LONS] + over
        tendency = (
            -0.5 * zonal[r : r + 1, :] * (lon_next - lon_prev)
            + LATERAL_MIX * (lon_next + lon_prev + lat_next + lat_prev - 4.0 * x)
            + VERTICAL_MIX * (vertical - 2.0 * x)
        )
        out[pl.ds(r, members, stride=ROWS), :] = x + ocean[lon] * tendency


def room(mebibytes):
    return pltpu.CompilerParams(vmem_limit_bytes=mebibytes * 1024 * 1024)


def swapped(x, axis, bit):
    return lax.ppermute(x, axis, [(i, i ^ bit) for i in range(lax.axis_size(axis))])


def shifted(x, axis, by):
    count = lax.axis_size(axis)
    return lax.ppermute(x, axis, [(i, (i + by) % count) for i in range(count)])


def local(state, observation_site, obs_count, measured_values, observation_noise, loc_pattern, ocean_mask, zonal_current):
    members = state.shape[0]
    columns = lax.axis_size("col")
    floors = lax.axis_size("gz")
    vmem = pl.BlockSpec(memory_space=pltpu.VMEM)
    smem = pl.BlockSpec(memory_space=pltpu.SMEM)
    height = members + 8
    level = members * LONS
    edge = members * LEVS + 8
    flat = state.reshape(members * ROWS, LATS)

    def like(*lengths):
        return [pltpu.VMEM((length, LATS), F32) for length in lengths]

    kept, core_send, y_send, inner, outer, own = pl.pallas_call(
        functools.partial(pick_kernel, members, columns),
        out_shape=like(height, height + level, level, edge, edge) + [pltpu.VMEM((ROWS, members, LATS), F32)],
        in_specs=[smem] + [vmem] * 6,
        out_specs=[vmem] * 6,
        name="pick_priors",
    )(
        obs_count.reshape(1, BATCHES),
        loc_pattern.reshape(BATCHES, 1, columns),
        observation_site,
        measured_values,
        observation_noise,
        ocean_mask,
        flat,
    )

    core_edge = swapped(core_send, "gz", 1)
    mine = kept + core_edge[:height]
    for bit in range(2, floors, 2):
        mine = mine + swapped(mine, "gz", bit)
    if columns <= 2 * WINDOW + 1 and columns & (columns - 1) == 0:
        around = None
        inner = swapped(jnp.concatenate([mine, inner]), "col", 1)
        pair = jnp.stack([mine, inner[:height]])
        gathered = [pair] + [swapped(pair, "col", bit) for bit in range(2, columns, 2)]
    else:
        inner = swapped(inner, "col", 1)
        around = tuple(range(-WINDOW, WINDOW + 1)) if columns > 2 * WINDOW + 1 else tuple(range(columns))
        gathered = [(mine if by == 0 else shifted(mine, "col", -by))[None] for by in around]

    ends = [(i, i + 1) for i in range(1, floors - 1, 2)]
    ends += [(j, i) for i, j in ends]
    ends += [(i, i) for i in range(floors) if i not in dict(ends)]
    y_edge = lax.ppermute(y_send, "gz", ends)
    ring = [(i, (i + 1) % columns) for i in range(1, columns, 2)]
    outer = lax.ppermute(outer, "col", ring + [(j, i) for i, j in ring])

    parts = tuple(part.shape[0] for part in gathered)
    other = [swapped(part, "gz", 1) for part in gathered]

    slots = min(sum(parts) * CAP, MEAN_COUNT * columns)
    chunks = -(-slots // CHUNK)
    rows = Y_ROW + 2 * chunks
    several = chunks > 1
    count = BATCHES * chunks
    limit = room(48 if several else 16)
    near, *terms = pl.pallas_call(
        functools.partial(near_kernel, members, parts, columns, around, chunks),
        out_shape=[
            pltpu.VMEM((rows, members, LATS), F32),
            pltpu.VMEM((count, CHUNK, CHUNK), BF16),
            pltpu.VMEM((count, 2 * members, CHUNK), BF16),
            pltpu.VMEM((count, CHUNK, LATS), F32),
            pltpu.VMEM((count, CHUNK, LATS), F32),
        ],
        in_specs=[vmem] * (4 + 2 * len(parts)),
        out_specs=[vmem] * 5,
        scratch_shapes=[
            pltpu.VMEM((BATCHES, chunks * CHUNK // CAP, height, CAP), F32),
            pltpu.VMEM((Y_ROW if several else 1, members, LATS), F32),
        ],
        compiler_params=limit,
        cost_estimate=pl.CostEstimate(flops=0, bytes_accessed=0, transcendentals=0),
        name="analyse_near",
    )(ocean_mask, own, core_edge, inner, *gathered, *other)
    out = pl.pallas_call(
        functools.partial(far_kernel, members, columns, floors, chunks),
        out_shape=jax.ShapeDtypeStruct((members * ROWS, LATS), F32),
        in_specs=[vmem] * 9,
        out_specs=vmem,
        scratch_shapes=[
            pltpu.VMEM((EXT_ROWS - Y_ROW, members, LATS), F32),
            pltpu.VMEM((EXT_ROWS - Y_ROW if several else 1, members, LATS), F32),
        ],
        compiler_params=limit,
        name="analyse_far_and_step",
    )(ocean_mask, zonal_current.reshape(ROWS, LATS), near, y_edge, outer, *terms)
    return out.reshape(state.shape)


def solution(mesh):
    in_specs = (
        P(None, "gz", "col", None),
        P(),
        P(None, "col"),
        P(None, "col"),
        P(None, "col"),
        P(None, None, "col"),
        P("col", None),
        P("gz", "col", None),
    )
    out_specs = P(None, "gz", "col", None)
    return jax.shard_map(local, mesh=mesh, in_specs=in_specs, out_specs=out_specs, check_vma=False)
```

```python
import functools

import jax
import jax.numpy as jnp
from jax import lax
from jax.experimental import pallas as pl
from jax.experimental.pallas import tpu as pltpu
from jax.sharding import PartitionSpec as P

LEVS = 2
LONS = 8
LATS = 128
BATCHES = 2
REACH = 3
CAP = 128
MEAN_COUNT = 32
WINDOW = 2 * REACH + 1
CHUNK = 256

CELLS = LEVS * LONS * LATS
ROWS = LEVS * LONS
CORE_ROW = 16
INNER_ROW = 24
Y_ROW = 26
OUTER_ROW = 34
EXT_ROWS = 36
ROW_LIMIT = 40
ROW_COLUMN = 24

LATERAL_MIX = 0.2
VERTICAL_MIX = 0.15

F32 = jnp.float32
BF16 = jnp.bfloat16


def iota(shape, dim):
    return lax.broadcasted_iota(jnp.int32, shape, dim)


def halves(x):
    high = x.astype(BF16)
    return high, (x - high.astype(F32)).astype(BF16)


def dot(a, b):
    return lax.dot_general(a, b, (((1,), (0,)), ((), ())), preferred_element_type=F32)


def dot_lanes(a, b):
    return lax.dot_general(a, b, (((1,), (1,)), ((), ())), preferred_element_type=F32)


def for_each(count, body):
    if count == 1:
        body(0)
    else:
        lax.fori_loop(0, count, lambda i, unused: (body(i), unused)[1], 0)


def rows_of(members):
    names = ("mask", "value", "noise", "links", "site", "occupied", "owner", "count")
    return {name: members + i for i, name in enumerate(names)}


def position():
    return lax.axis_index("col").astype(jnp.int32), lax.axis_index("gz").astype(jnp.int32)


def pick_kernel(members, columns, count, linked, site, value, noise, mask, state, kept, core_send, y_send, inner, outer, rows):
    col, gz = position()
    core = gz % 2
    lane = iota((1, CAP), 1)
    at = pl.multiple_of(col * CAP, CAP)
    index, filled = [], []
    for b in range(BATCHES):
        occupied = lane < count[0, b]
        filled.append(occupied)
        index.append(jnp.where(occupied, site[b : b + 1, pl.ds(at, CAP)] - gz * CELLS, -1))
    wanted = jnp.concatenate(index, 1)
    total = jnp.zeros((3 * members + 16, BATCHES * CAP), F32)
    cell = iota((2 * LATS, BATCHES * CAP), 0)
    ocean = mask[...].astype(F32)
    for pair in range(ROWS // 2):
        left = []
        for r in (2 * pair, 2 * pair + 1):
            x = state[pl.ds(r, members, stride=ROWS), :]
            rows[r] = x
            high = x.astype(BF16)
            rest = x - high.astype(F32)
            middle = rest.astype(BF16)
            low = (rest - middle.astype(F32)).astype(BF16)
            lon = r % LONS
            row = jnp.broadcast_to(ocean[lon : lon + 1, :], (16, LATS)).astype(BF16)
            left.append(jnp.concatenate([high, row, middle, low], 0))
        hit = jnp.where(cell + pair * 2 * LATS == wanted, 1.0, 0.0).astype(BF16)
        total = total + dot(jnp.concatenate(left, 1), hit)
    m = members
    height = m + 8
    picked = (total[:m] + total[m + 16 : 2 * m + 16]) + total[2 * m + 16 :]
    first = jnp.where(gz == 0, 1.0, 0.0)
    for b in range(BATCHES):
        here = slice(b * CAP, (b + 1) * CAP)
        once = jnp.where(filled[b], first, 0.0)
        links = jnp.concatenate([linked[b].astype(F32), jnp.zeros((1, CAP - columns), F32)], 1)
        tail = [
            total[m : m + 1, here],
            value[b : b + 1, :] * once,
            noise[b : b + 1, :] * once,
            links * first,
            site[b : b + 1, pl.ds(at, CAP)].astype(F32) * once,
            once,
            once * col.astype(F32),
            jnp.full((1, CAP), count[0, b].astype(F32) * first),
        ]
        block = jnp.concatenate([picked[:, here]] + tail, 0)

        @pl.when(core == b)
        def _():
            kept[...] = block

        @pl.when(core != b)
        def _():
            core_send[:height, :] = block

    for member in range(members):
        up = state[pl.ds(pl.multiple_of(member * ROWS + (1 - core) * LONS, LONS), LONS), :]
        core_send[height + member * LONS : height + (member + 1) * LONS, :] = up
        down = state[pl.ds(pl.multiple_of(member * ROWS + core * LONS, LONS), LONS), :]
        y_send[member * LONS : (member + 1) * LONS, :] = down
    even = col % 2 == 0
    for lev in range(LEVS):
        west = state[pl.ds(lev * LONS, members, stride=ROWS), :]
        east = state[pl.ds(lev * LONS + LONS - 1, members, stride=ROWS), :]
        inner[lev * members : (lev + 1) * members, :] = jnp.where(even, east, west)
        outer[lev * members : (lev + 1) * members, :] = jnp.where(even, west, east)
    west = jnp.broadcast_to(ocean[:1], (8, LATS))
    east = jnp.broadcast_to(ocean[LONS - 1 :], (8, LATS))
    inner[LEVS * members :, :] = jnp.where(even, east, west)
    outer[LEVS * members :, :] = jnp.where(even, west, east)


def place_terms(col, gz, columns):
    lon_all = columns * LONS
    odd = gz % 2
    even_col = col % 2 == 0
    at = iota((ROW_LIMIT, 1), 0)
    above, below = LEVS * gz + LEVS, LEVS * gz - 1
    own = at < ROWS
    near = (at >= CORE_ROW) & (at < INNER_ROW)
    far = (at >= Y_ROW) & (at < OUTER_ROW)
    row_lev = LEVS * gz + jnp.where(own, at // LONS, at % LEVS)
    row_lev = jnp.where(near, jnp.where(odd == 0, above, below), row_lev)
    row_lev = jnp.where(far, jnp.where(odd == 0, below, above), row_lev)
    west_lon = (col * LONS + lon_all - 1) % lon_all
    east_lon = (col * LONS + LONS) % lon_all
    inner = (at >= INNER_ROW) & (at < Y_ROW)
    row_lon = col * LONS + jnp.where(far, at - Y_ROW, at % LONS)
    row_lon = jnp.where(inner, jnp.where(even_col, east_lon, west_lon), row_lon)
    row_lon = jnp.where(at >= OUTER_ROW, jnp.where(even_col, west_lon, east_lon), row_lon)
    west_col = (col + columns - 1) % columns
    east_col = (col + 1) % columns
    inner_col = jnp.where(even_col, east_col, west_col)
    outer_col = jnp.where(even_col, west_col, east_col)
    return row_lev.astype(F32), row_lon.astype(F32), inner, at >= OUTER_ROW, inner_col, outer_col


def centred_parts(x):
    x = x - jnp.sum(x, 0, keepdims=True) * (1.0 / x.shape[0])
    high, low = halves(x)
    return jnp.concatenate([high, low, high, jnp.zeros((16, x.shape[1]), BF16)], 0)


def increment(x, sides, gains, local):
    members = x.shape[0]
    weighted = dot(sides, centred_parts(x)) * local
    high, low = halves(weighted)
    first = dot(gains, high)
    return (first[:members] + first[members:]) + dot(gains[:members], low)


def move_rows(fields, gained, first, last, ocean, terms, b, chunks):
    sides, gains, row_part, lat_part = terms

    def chunk(k):
        t = b * chunks + k
        for r in range(first, last, 2):
            at = r - first
            x = jnp.concatenate([fields[at], fields[at + 1]], 1)
            columns = [ROW_COLUMN + r + h for h in range(2)]
            tapers = [lat_part[t] * row_part[t, :, c : c + 1] for c in columns]
            moved = increment(x, sides[t], gains[t], jnp.concatenate(tapers, 1))
            moved = moved * jnp.concatenate([ocean[at], ocean[at + 1]], 1)
            for h in range(2):
                piece = slice(h * LATS, (h + 1) * LATS)
                if chunks == 1:
                    fields[at + h] = x[:, piece] + moved[:, piece]
                else:
                    gained[at + h] = gained[at + h] + moved[:, piece]

    if chunks > 1:
        gained[...] = jnp.zeros_like(gained)
    for_each(chunks, chunk)
    if chunks > 1:
        for at in range(last - first):
            fields[at] = fields[at] + gained[at]


def near_kernel(members, parts, columns, flip, around, chunks, mask, own, core_edge, inner, *rest):
    mine_parts, other_parts = rest[: len(parts)], rest[len(parts) : 2 * len(parts)]
    fields, sides, gains, row_terms, lat_terms, packed, gained = rest[2 * len(parts) :]
    mine = [part.at[i] for part, size in zip(mine_parts, parts) for i in range(size)]
    other = [part.at[i] for part, size in zip(other_parts, parts) for i in range(size)]
    blocks = len(mine)
    col, gz = position()
    core = gz % 2
    lon_all = columns * LONS
    place = rows_of(members)
    denominator = 1.0 / (members - 1)
    height = members + 8
    owners = [col ^ i if flip else (col + i + columns) % columns for i in around]

    lane = iota((1, LATS), 1)
    pad = (-blocks) % 16
    tables = []
    for b in range(BATCHES):
        start = jnp.zeros((1, CAP), jnp.int32)
        tiles = [jnp.zeros((height, CAP), F32)] * (chunks * CHUNK // CAP)
        links = []
        for j in range(blocks):
            block = jnp.where(core == b, mine[j][...], other[j][...])
            links.append(block[place["links"] : place["links"] + 1, :])
            if j == 0:
                tiles[0] = block
            else:
                shift = start % CAP
                turned = pltpu.roll(block, shift[0, 0], 1)
                into = start // CAP + jnp.where(lane < shift, 1, 0)
                tiles = [tile + jnp.where(into == i, turned, 0.0) for i, tile in enumerate(tiles)]
            start = start + block[place["count"] : place["count"] + 1, :].astype(jnp.int32)
        for i, tile in enumerate(tiles):
            packed[b, i] = tile
        tables.append(jnp.concatenate(links + [jnp.zeros((pad, CAP), F32)] * (pad > 0), 0).astype(BF16))

    inner_start = inner.shape[0] - (members * LEVS + 8)
    for r in range(ROWS):
        fields[r] = own[r]
    for lon in range(LONS):
        fields[CORE_ROW + lon] = core_edge[pl.ds(height + lon, members, stride=LONS), :]
    for lev in range(LEVS):
        at = inner_start + lev * members
        fields[INNER_ROW + lev] = inner[at : at + members, :]
    wet = mask[...].astype(F32)
    ocean = [wet[lon : lon + 1] for lon in range(LONS)] * 3
    at = inner_start + members * LEVS
    ocean += [inner[at : at + 1, :]] * LEVS

    row_lev, row_lon, inside, outside, inner_col, outer_col = place_terms(col, gz, columns)

    def places(site, owner):
        site = site.astype(jnp.int32)
        lev = site // (LONS * LATS)
        lon = owner.astype(jnp.int32) * LONS + site // LATS % LONS
        return lev.astype(F32), lon.astype(F32), (site % LATS).astype(F32)

    def lon_square(a, b):
        gap = jnp.abs(a - b)
        gap = jnp.minimum(gap, lon_all - gap) * (1.0 / (2.0 * LONS))
        return 1.0 + gap * gap

    def lev_square(a, b):
        gap = (a - b) * 0.5
        return 1.0 + gap * gap

    def lat_square(a, b):
        gap = (a - b) * (1.0 / (LATS // 8))
        return 1.0 + gap * gap

    def slots_of(b, k):
        wide = jnp.concatenate([packed[b, 2 * k], packed[b, 2 * k + 1]], 1)

        def row(name):
            return wide[place[name] : place[name] + 1]

        return wide, row

    def batch_terms(b, k):
        wide, row = slots_of(b, k)
        occupied = row("occupied")
        if b == 0:
            prior = wide[:members]
        else:
            prior = jnp.concatenate([fields[Y_ROW + 2 * k], fields[Y_ROW + 2 * k + 1]], 1) * occupied
        noise = jnp.where(occupied > 0, row("noise"), 1.0)
        mean = jnp.sum(prior, 0, keepdims=True) / members
        anomaly = prior - mean
        spread = jnp.sum(anomaly * anomaly, 0, keepdims=True) * denominator
        total = spread + noise
        shrink = 1.0 / (1.0 + jnp.sqrt(noise / total))
        gain = ((row("value") - mean) - shrink * anomaly) / total
        high = anomaly.astype(BF16).astype(F32)
        stack = jnp.concatenate([high, high, anomaly - high, jnp.zeros((16, CHUNK), F32)], 0)
        t = b * chunks + k
        sides[t] = stack.T.astype(BF16)
        gains[t] = jnp.concatenate(halves(gain), 0)

    def batch_tapers(b, k):
        wide, row = slots_of(b, k)
        owner = row("owner")
        lev, lon, lat = places(row("site"), owner)
        holder = jnp.where(iota((CAP, CHUNK), 0).astype(F32) == owner, 1.0, 0.0).astype(BF16)
        by_block = dot(tables[b], holder)
        weight = []
        for target in (col, inner_col, outer_col):
            total = jnp.zeros((1, CHUNK), F32)
            for j in range(blocks):
                total = total + jnp.where(owners[j] == target, by_block[j : j + 1], 0.0)
            weight.append(total)
        weight = jnp.where(inside, weight[1], jnp.where(outside, weight[2], weight[0]))
        weight = weight * denominator / (lev_square(row_lev, lev) * lon_square(row_lon, lon))
        spare = LATS - ROW_COLUMN - ROW_LIMIT
        table = jnp.concatenate(
            [lat, lev, lon, jnp.zeros((5, CHUNK), F32), by_block[:16], weight, jnp.zeros((spare, CHUNK), F32)], 0
        )
        t = b * chunks + k
        row_terms[t] = table.T
        lat_terms[t] = 1.0 / lat_square(lane.astype(F32), row_terms[t, :, 0:1])

    def site_weights(k0, k1):
        wide, row = slots_of(1, k1)
        owner = row("owner")
        lev, lon, lat = places(row("site"), owner)
        there = [jnp.where(owner == owners[j].astype(F32), 1.0, 0.0) for j in range(blocks)]
        there += [jnp.zeros((pad, CHUNK), F32)] * (pad > 0)
        weight = dot(row_terms[k0, :, 8:24].astype(BF16), jnp.concatenate(there, 0).astype(BF16))
        lat0, lev0, lon0 = [row_terms[k0, :, i : i + 1] for i in range(3)]
        square = lat_square(lat0, lat) * lon_square(lon0, lon) * lev_square(lev0, lev)
        return weight * denominator / square, wide

    def first_terms(k):
        batch_terms(0, k)
        batch_tapers(0, k)

        def site_chunk(k1):
            taper, wide = site_weights(k, k1)
            x = wide[:members]
            moved = increment(x, sides[k], gains[k], taper) * wide[members : members + 1]
            for h in range(2):
                at = Y_ROW + 2 * k1 + h
                piece = slice(h * LATS, (h + 1) * LATS)
                before = x[:, piece] if chunks == 1 else jnp.where(k == 0, x[:, piece], fields[at])
                fields[at] = before + moved[:, piece]

        for_each(chunks, site_chunk)

    def second_terms(k):
        batch_terms(1, k)
        batch_tapers(1, k)

    terms = (sides, gains, row_terms, lat_terms)
    for_each(chunks, first_terms)
    for_each(chunks, second_terms)
    for b in range(BATCHES):
        move_rows(fields, gained, 0, Y_ROW, ocean, terms, b, chunks)


def far_kernel(
    members, columns, floors, chunks, mask, zonal, near, y_edge, outer, sides, gains, row_terms, lat_terms, out, fields, gained
):
    col, gz = position()
    core = gz % 2
    even_col = col % 2 == 0
    lane = iota((1, LATS), 1)
    outer_at = OUTER_ROW - Y_ROW
    beyond = gz + 2 * core - 1
    inside = jnp.where((beyond >= 0) & (beyond < floors), 1.0, 0.0)
    for lon in range(LONS):
        fields[lon] = y_edge[pl.ds(lon, members, stride=LONS), :] * inside
    for lev in range(LEVS):
        fields[outer_at + lev] = outer[lev * members : (lev + 1) * members, :]
    wet = mask[...].astype(F32)
    ocean = [wet[lon : lon + 1] for lon in range(LONS)]
    edge = members * LEVS
    terms = (sides, gains, row_terms, lat_terms)
    for b in range(BATCHES):
        move_rows(fields, gained, Y_ROW, EXT_ROWS, ocean + [outer[edge : edge + 1, :]] * LEVS, terms, b, chunks)

    for r in range(ROWS):
        lev, lon = r // LONS, r % LONS
        x = near[r]
        side = [near[INNER_ROW + lev], fields[outer_at + lev]]
        lon_next = near[r + 1] if lon < LONS - 1 else jnp.where(even_col, side[0], side[1])
        lon_prev = near[r - 1] if lon > 0 else jnp.where(even_col, side[1], side[0])
        lat_next = jnp.where(lane < LATS - 1, pltpu.roll(x, LATS - 1, 1), 0.0)
        lat_prev = jnp.where(lane > 0, pltpu.roll(x, 1, 1), 0.0)
        over = jnp.where(core == 1 - lev, near[CORE_ROW + lon], fields[lon])
        vertical = near[r ^ LONS] + over
        tendency = (
            -0.5 * zonal[r : r + 1, :] * (lon_next - lon_prev)
            + LATERAL_MIX * (lon_next + lon_prev + lat_next + lat_prev - 4.0 * x)
            + VERTICAL_MIX * (vertical - 2.0 * x)
        )
        out[pl.ds(r, members, stride=ROWS), :] = x + ocean[lon] * tendency


def room(mebibytes):
    return pltpu.CompilerParams(vmem_limit_bytes=mebibytes * 1024 * 1024)


def swapped(x, axis, bit):
    return lax.ppermute(x, axis, [(i, i ^ bit) for i in range(lax.axis_size(axis))])


def shifted(x, axis, by):
    count = lax.axis_size(axis)
    return lax.ppermute(x, axis, [(i, (i + by) % count) for i in range(count)])


def local(state, observation_site, obs_count, measured_values, observation_noise, loc_pattern, ocean_mask, zonal_current):
    members = state.shape[0]
    columns = lax.axis_size("col")
    floors = lax.axis_size("gz")
    vmem = pl.BlockSpec(memory_space=pltpu.VMEM)
    smem = pl.BlockSpec(memory_space=pltpu.SMEM)
    height = members + 8
    level = members * LONS
    edge = members * LEVS + 8
    flat = state.reshape(members * ROWS, LATS)

    def like(*lengths):
        return [pltpu.VMEM((length, LATS), F32) for length in lengths]

    kept, core_send, y_send, inner, outer, own = pl.pallas_call(
        functools.partial(pick_kernel, members, columns),
        out_shape=like(height, height + level, level, edge, edge) + [pltpu.VMEM((ROWS, members, LATS), F32)],
        in_specs=[smem] + [vmem] * 6,
        out_specs=[vmem] * 6,
        name="pick_priors",
    )(
        obs_count.reshape(1, BATCHES),
        loc_pattern.reshape(BATCHES, 1, columns),
        observation_site,
        measured_values,
        observation_noise,
        ocean_mask,
        flat,
    )

    core_edge = swapped(core_send, "gz", 1)
    mine = kept + core_edge[:height]
    for bit in range(2, floors, 2):
        mine = mine + swapped(mine, "gz", bit)
    flip = columns <= 2 * WINDOW + 1 and columns & (columns - 1) == 0
    if flip:
        inner = swapped(jnp.concatenate([mine, inner]), "col", 1)
        passed = [swapped(mine, "col", bit) for bit in range(2, columns, 2)]
        near = jnp.stack([mine, inner[:height]] + passed)
        gathered = [near, swapped(near[2:], "col", 1)]
        around = [0, 1] + list(range(2, columns, 2)) + list(range(3, columns, 2))
    else:
        inner = swapped(inner, "col", 1)
        around = tuple(range(-WINDOW, WINDOW + 1)) if columns > 2 * WINDOW + 1 else tuple(range(columns))
        gathered = [(mine if by == 0 else shifted(mine, "col", -by))[None] for by in around]

    ends = [(i, i + 1) for i in range(1, floors - 1, 2)]
    ends += [(j, i) for i, j in ends]
    ends += [(i, i) for i in range(floors) if i not in dict(ends)]
    y_edge = lax.ppermute(y_send, "gz", ends)
    ring = [(i, (i + 1) % columns) for i in range(1, columns, 2)]
    outer = lax.ppermute(outer, "col", ring + [(j, i) for i, j in ring])

    parts = tuple(part.shape[0] for part in gathered)
    other = [swapped(part, "gz", 1) for part in gathered]

    slots = min(sum(parts) * CAP, MEAN_COUNT * columns)
    chunks = -(-slots // CHUNK)
    rows = Y_ROW + 2 * chunks
    several = chunks > 1
    count = BATCHES * chunks
    limit = room(48 if several else 16)
    near, *terms = pl.pallas_call(
        functools.partial(near_kernel, members, parts, columns, flip, around, chunks),
        out_shape=[
            pltpu.VMEM((rows, members, LATS), F32),
            pltpu.VMEM((count, CHUNK, CHUNK), BF16),
            pltpu.VMEM((count, 2 * members, CHUNK), BF16),
            pltpu.VMEM((count, CHUNK, LATS), F32),
            pltpu.VMEM((count, CHUNK, LATS), F32),
        ],
        in_specs=[vmem] * (4 + 2 * len(parts)),
        out_specs=[vmem] * 5,
        scratch_shapes=[
            pltpu.VMEM((BATCHES, chunks * CHUNK // CAP, height, CAP), F32),
            pltpu.VMEM((Y_ROW if several else 1, members, LATS), F32),
        ],
        compiler_params=limit,
        cost_estimate=pl.CostEstimate(flops=0, bytes_accessed=0, transcendentals=0),
        name="analyse_near",
    )(ocean_mask, own, core_edge, inner, *gathered, *other)
    out = pl.pallas_call(
        functools.partial(far_kernel, members, columns, floors, chunks),
        out_shape=jax.ShapeDtypeStruct((members * ROWS, LATS), F32),
        in_specs=[vmem] * 9,
        out_specs=vmem,
        scratch_shapes=[
            pltpu.VMEM((EXT_ROWS - Y_ROW, members, LATS), F32),
            pltpu.VMEM((EXT_ROWS - Y_ROW if several else 1, members, LATS), F32),
        ],
        compiler_params=limit,
        name="analyse_far_and_step",
    )(ocean_mask, zonal_current.reshape(ROWS, LATS), near, y_edge, outer, *terms)
    return out.reshape(state.shape)


def solution(mesh):
    in_specs = (
        P(None, "gz", "col", None),
        P(),
        P(None, "col"),
        P(None, "col"),
        P(None, "col"),
        P(None, None, "col"),
        P("col", None),
        P("gz", "col", None),
    )
    out_specs = P(None, "gz", "col", None)
    return jax.shard_map(local, mesh=mesh, in_specs=in_specs, out_specs=out_specs, check_vma=False)
```

```python
import functools

import jax
import jax.numpy as jnp
from jax import lax
from jax.experimental import pallas as pl
from jax.experimental.pallas import tpu as pltpu
from jax.sharding import PartitionSpec as P

LEVS = 2
LONS = 8
LATS = 128
BATCHES = 2
REACH = 3
CAP = 128
MEAN_COUNT = 32
WINDOW = 2 * REACH + 1
CHUNK = 256

CELLS = LEVS * LONS * LATS
ROWS = LEVS * LONS
CORE_ROW = 16
INNER_ROW = 24
Y_ROW = 26
OUTER_ROW = 34
EXT_ROWS = 36
ROW_LIMIT = 40
ROW_COLUMN = 24

LATERAL_MIX = 0.2
VERTICAL_MIX = 0.15

F32 = jnp.float32
BF16 = jnp.bfloat16


def iota(shape, dim):
    return lax.broadcasted_iota(jnp.int32, shape, dim)


def halves(x):
    high = x.astype(BF16)
    return high, (x - high.astype(F32)).astype(BF16)


def dot(a, b):
    return lax.dot_general(a, b, (((1,), (0,)), ((), ())), preferred_element_type=F32)


def dot_lanes(a, b):
    return lax.dot_general(a, b, (((1,), (1,)), ((), ())), preferred_element_type=F32)


def for_each(count, body):
    if count == 1:
        body(0)
    else:
        lax.fori_loop(0, count, lambda i, unused: (body(i), unused)[1], 0)


def rows_of(members):
    names = ("mask", "value", "noise", "links", "site", "occupied", "owner", "count")
    return {name: members + i for i, name in enumerate(names)}


def position():
    return lax.axis_index("col").astype(jnp.int32), lax.axis_index("gz").astype(jnp.int32)


def pick_kernel(members, columns, count, linked, site, value, noise, mask, state, kept, given):
    col, gz = position()
    core = gz % 2
    lane = iota((1, CAP), 1)
    at = pl.multiple_of(col * CAP, CAP)
    index, filled = [], []
    for b in range(BATCHES):
        occupied = lane < count[0, b]
        filled.append(occupied)
        index.append(jnp.where(occupied, site[b : b + 1, pl.ds(at, CAP)] - gz * CELLS, -1))
    wanted = jnp.concatenate(index, 1)
    total = jnp.zeros((3 * members + 16, BATCHES * CAP), F32)
    cell = iota((2 * LATS, BATCHES * CAP), 0)
    ocean = mask[...].astype(F32)
    for pair in range(ROWS // 2):
        left = []
        for r in (2 * pair, 2 * pair + 1):
            x = state[pl.ds(r, members, stride=ROWS), :]
            high = x.astype(BF16)
            rest = x - high.astype(F32)
            middle = rest.astype(BF16)
            low = (rest - middle.astype(F32)).astype(BF16)
            lon = r % LONS
            row = jnp.broadcast_to(ocean[lon : lon + 1, :], (16, LATS)).astype(BF16)
            left.append(jnp.concatenate([high, row, middle, low], 0))
        hit = jnp.where(cell + pair * 2 * LATS == wanted, 1.0, 0.0).astype(BF16)
        total = total + dot(jnp.concatenate(left, 1), hit)
    m = members
    picked = (total[:m] + total[m + 16 : 2 * m + 16]) + total[2 * m + 16 :]
    first = jnp.where(gz == 0, 1.0, 0.0)
    for b in range(BATCHES):
        here = slice(b * CAP, (b + 1) * CAP)
        once = jnp.where(filled[b], first, 0.0)
        links = jnp.concatenate([linked[b].astype(F32), jnp.zeros((1, CAP - columns), F32)], 1)
        tail = [
            total[m : m + 1, here],
            value[b : b + 1, :] * once,
            noise[b : b + 1, :] * once,
            links * first,
            site[b : b + 1, pl.ds(at, CAP)].astype(F32) * once,
            once,
            once * col.astype(F32),
            jnp.full((1, CAP), count[0, b].astype(F32) * first),
        ]
        block = jnp.concatenate([picked[:, here]] + tail, 0)

        @pl.when(core == b)
        def _():
            kept[...] = block

        @pl.when(core != b)
        def _():
            given[...] = block


def edges_kernel(members, mask, state, core_send, y_send, inner, outer, rows):
    col, gz = position()
    core = gz % 2
    ocean = mask[...].astype(F32)
    for r in range(ROWS):
        rows[r] = state[pl.ds(r, members, stride=ROWS), :]
    for member in range(members):
        to = slice(member * LONS, (member + 1) * LONS)
        core_send[to, :] = state[pl.ds(pl.multiple_of(member * ROWS + (1 - core) * LONS, LONS), LONS), :]
        y_send[to, :] = state[pl.ds(pl.multiple_of(member * ROWS + core * LONS, LONS), LONS), :]
    even = col % 2 == 0
    for lev in range(LEVS):
        west, east = rows[lev * LONS], rows[lev * LONS + LONS - 1]
        to = slice(lev * members, (lev + 1) * members)
        inner[to, :] = jnp.where(even, east, west)
        outer[to, :] = jnp.where(even, west, east)
    west = jnp.broadcast_to(ocean[:1], (8, LATS))
    east = jnp.broadcast_to(ocean[LONS - 1 :], (8, LATS))
    inner[LEVS * members :, :] = jnp.where(even, east, west)
    outer[LEVS * members :, :] = jnp.where(even, west, east)


def place_terms(col, gz, columns):
    lon_all = columns * LONS
    odd = gz % 2
    even_col = col % 2 == 0
    at = iota((ROW_LIMIT, 1), 0)
    above, below = LEVS * gz + LEVS, LEVS * gz - 1
    own = at < ROWS
    near = (at >= CORE_ROW) & (at < INNER_ROW)
    far = (at >= Y_ROW) & (at < OUTER_ROW)
    row_lev = LEVS * gz + jnp.where(own, at // LONS, at % LEVS)
    row_lev = jnp.where(near, jnp.where(odd == 0, above, below), row_lev)
    row_lev = jnp.where(far, jnp.where(odd == 0, below, above), row_lev)
    west_lon = (col * LONS + lon_all - 1) % lon_all
    east_lon = (col * LONS + LONS) % lon_all
    inner = (at >= INNER_ROW) & (at < Y_ROW)
    row_lon = col * LONS + jnp.where(far, at - Y_ROW, at % LONS)
    row_lon = jnp.where(inner, jnp.where(even_col, east_lon, west_lon), row_lon)
    row_lon = jnp.where(at >= OUTER_ROW, jnp.where(even_col, west_lon, east_lon), row_lon)
    west_col = (col + columns - 1) % columns
    east_col = (col + 1) % columns
    inner_col = jnp.where(even_col, east_col, west_col)
    outer_col = jnp.where(even_col, west_col, east_col)
    return row_lev.astype(F32), row_lon.astype(F32), inner, at >= OUTER_ROW, inner_col, outer_col


def centred_parts(x):
    x = x - jnp.sum(x, 0, keepdims=True) * (1.0 / x.shape[0])
    high, low = halves(x)
    return jnp.concatenate([high, low, high, jnp.zeros((16, x.shape[1]), BF16)], 0)


def products(covariance, local, gains):
    members = gains.shape[0] // 2
    high, low = halves(covariance * local)
    return dot(gains, high), dot(gains[:members], low)


def added(first, second):
    members = second.shape[0]
    return (first[:members] + first[members:]) + second


def increment(x, sides, gains, local):
    return added(*products(dot(sides, centred_parts(x)), local, gains))


def move_pairs(fields, into, first, last, ocean, terms, steps, meanwhile=None):
    sides, gains, row_part, lat_part = terms
    ahead = []

    def finish():
        t, at, x, covariance = ahead.pop(0)
        columns = [ROW_COLUMN + first + at + h for h in range(2)]
        tapers = [lat_part[t] * row_part[t, :, c : c + 1] for c in columns]
        moved = added(*products(covariance, jnp.concatenate(tapers, 1), gains[t]))
        moved = moved * jnp.concatenate([ocean[at], ocean[at + 1]], 1)
        for h in range(2):
            piece = slice(h * LATS, (h + 1) * LATS)
            if into is fields:
                fields[at + h] = x[:, piece] + moved[:, piece]
            else:
                into[at + h] = into[at + h] + moved[:, piece]

    for i, (t, at) in enumerate([(t, at) for t in steps for at in range(0, last - first, 2)]):
        if meanwhile is not None and i == meanwhile[0]:
            meanwhile[1]()
        x = jnp.concatenate([fields[at], fields[at + 1]], 1)
        ahead.append((t, at, x, dot(sides[t], centred_parts(x))))
        if len(ahead) > 1:
            finish()
    finish()


def move_rows(fields, gained, first, last, ocean, terms, chunks, meanwhile=None):
    if chunks == 1:
        move_pairs(fields, fields, first, last, ocean, terms, range(BATCHES), meanwhile)
        return
    if meanwhile is not None:
        meanwhile[1]()
    for b in range(BATCHES):
        gained[...] = jnp.zeros_like(gained)
        for_each(chunks, lambda k: move_pairs(fields, gained, first, last, ocean, terms, [b * chunks + k]))
        for at in range(last - first):
            fields[at] = fields[at] + gained[at]


def near_kernel(members, parts, columns, flip, around, chunks, mask, own, core_edge, inner, *rest):
    mine_parts, other_parts = rest[: len(parts)], rest[len(parts) : 2 * len(parts)]
    fields, sides, gains, row_terms, lat_terms, packed, gained = rest[2 * len(parts) :]
    mine = [part.at[i] for part, size in zip(mine_parts, parts) for i in range(size)]
    other = [part.at[i] for part, size in zip(other_parts, parts) for i in range(size)]
    blocks = len(mine)
    col, gz = position()
    core = gz % 2
    lon_all = columns * LONS
    place = rows_of(members)
    denominator = 1.0 / (members - 1)
    height = members + 8
    owners = [col ^ i if flip else (col + i + columns) % columns for i in around]

    lane = iota((1, LATS), 1)
    pad = (-blocks) % 16
    tables = []
    for b in range(BATCHES):
        start = jnp.zeros((1, CAP), jnp.int32)
        tiles = [jnp.zeros((height, CAP), F32)] * (chunks * CHUNK // CAP)
        links = []
        for j in range(blocks):
            block = jnp.where(core == b, mine[j][...], other[j][...])
            links.append(block[place["links"] : place["links"] + 1, :])
            if j == 0:
                tiles[0] = block
            else:
                shift = start % CAP
                turned = pltpu.roll(block, shift[0, 0], 1)
                into = start // CAP + jnp.where(lane < shift, 1, 0)
                tiles = [tile + jnp.where(into == i, turned, 0.0) for i, tile in enumerate(tiles)]
            start = start + block[place["count"] : place["count"] + 1, :].astype(jnp.int32)
        for i, tile in enumerate(tiles):
            packed[b, i] = tile
        tables.append(jnp.concatenate(links + [jnp.zeros((pad, CAP), F32)] * (pad > 0), 0).astype(BF16))

    inner_start = inner.shape[0] - (members * LEVS + 8)
    for r in range(ROWS):
        fields[r] = own[r]
    for lon in range(LONS):
        fields[CORE_ROW + lon] = core_edge[pl.ds(lon, members, stride=LONS), :]
    for lev in range(LEVS):
        at = inner_start + lev * members
        fields[INNER_ROW + lev] = inner[at : at + members, :]
    wet = mask[...].astype(F32)
    ocean = [wet[lon : lon + 1] for lon in range(LONS)] * 3
    at = inner_start + members * LEVS
    ocean += [inner[at : at + 1, :]] * LEVS

    row_lev, row_lon, inside, outside, inner_col, outer_col = place_terms(col, gz, columns)

    def places(site, owner):
        site = site.astype(jnp.int32)
        lev = site // (LONS * LATS)
        lon = owner.astype(jnp.int32) * LONS + site // LATS % LONS
        return lev.astype(F32), lon.astype(F32), (site % LATS).astype(F32)

    def lon_square(a, b):
        gap = jnp.abs(a - b)
        gap = jnp.minimum(gap, lon_all - gap) * (1.0 / (2.0 * LONS))
        return 1.0 + gap * gap

    def lev_square(a, b):
        gap = (a - b) * 0.5
        return 1.0 + gap * gap

    def lat_square(a, b):
        gap = (a - b) * (1.0 / (LATS // 8))
        return 1.0 + gap * gap

    def slots_of(b, k):
        wide = jnp.concatenate([packed[b, 2 * k], packed[b, 2 * k + 1]], 1)

        def row(name):
            return wide[place[name] : place[name] + 1]

        return wide, row

    def batch_terms(b, k):
        wide, row = slots_of(b, k)
        occupied = row("occupied")
        if b == 0:
            prior = wide[:members]
        else:
            prior = jnp.concatenate([fields[Y_ROW + 2 * k], fields[Y_ROW + 2 * k + 1]], 1) * occupied
        noise = jnp.where(occupied > 0, row("noise"), 1.0)
        mean = jnp.sum(prior, 0, keepdims=True) / members
        anomaly = prior - mean
        spread = jnp.sum(anomaly * anomaly, 0, keepdims=True) * denominator
        total = spread + noise
        shrink = 1.0 / (1.0 + jnp.sqrt(noise / total))
        gain = ((row("value") - mean) - shrink * anomaly) / total
        high = anomaly.astype(BF16).astype(F32)
        stack = jnp.concatenate([high, high, anomaly - high, jnp.zeros((16, CHUNK), F32)], 0)
        t = b * chunks + k
        sides[t] = stack.T.astype(BF16)
        gains[t] = jnp.concatenate(halves(gain), 0)

    def batch_tapers(b, k):
        wide, row = slots_of(b, k)
        owner = row("owner")
        lev, lon, lat = places(row("site"), owner)
        holder = jnp.where(iota((CAP, CHUNK), 0).astype(F32) == owner, 1.0, 0.0).astype(BF16)
        by_block = dot(tables[b], holder)
        weight = []
        for target in (col, inner_col, outer_col):
            total = jnp.zeros((1, CHUNK), F32)
            for j in range(blocks):
                total = total + jnp.where(owners[j] == target, by_block[j : j + 1], 0.0)
            weight.append(total)
        weight = jnp.where(inside, weight[1], jnp.where(outside, weight[2], weight[0]))
        weight = weight * denominator / (lev_square(row_lev, lev) * lon_square(row_lon, lon))
        spare = LATS - ROW_COLUMN - ROW_LIMIT
        table = jnp.concatenate(
            [lat, lev, lon, jnp.zeros((5, CHUNK), F32), by_block[:16], weight, jnp.zeros((spare, CHUNK), F32)], 0
        )
        t = b * chunks + k
        row_terms[t] = table.T
        lat_terms[t] = 1.0 / lat_square(lane.astype(F32), row_terms[t, :, 0:1])

    def site_weights(k0, k1):
        wide, row = slots_of(1, k1)
        owner = row("owner")
        lev, lon, lat = places(row("site"), owner)
        there = [jnp.where(owner == owners[j].astype(F32), 1.0, 0.0) for j in range(blocks)]
        there += [jnp.zeros((pad, CHUNK), F32)] * (pad > 0)
        weight = dot(row_terms[k0, :, 8:24].astype(BF16), jnp.concatenate(there, 0).astype(BF16))
        lat0, lev0, lon0 = [row_terms[k0, :, i : i + 1] for i in range(3)]
        square = lat_square(lat0, lat) * lon_square(lon0, lon) * lev_square(lev0, lev)
        return weight * denominator / square, wide

    def first_terms(k):
        batch_terms(0, k)
        batch_tapers(0, k)

        def site_chunk(k1):
            taper, wide = site_weights(k, k1)
            x = wide[:members]
            moved = increment(x, sides[k], gains[k], taper) * wide[members : members + 1]
            for h in range(2):
                at = Y_ROW + 2 * k1 + h
                piece = slice(h * LATS, (h + 1) * LATS)
                before = x[:, piece] if chunks == 1 else jnp.where(k == 0, x[:, piece], fields[at])
                fields[at] = before + moved[:, piece]

        for_each(chunks, site_chunk)

    def second_terms(k):
        batch_terms(1, k)
        batch_tapers(1, k)

    terms = (sides, gains, row_terms, lat_terms)
    for_each(chunks, first_terms)
    meanwhile = (6, lambda: for_each(chunks, second_terms))
    move_rows(fields, gained, 0, Y_ROW, ocean, terms, chunks, meanwhile)


def far_kernel(
    members, columns, floors, chunks, mask, zonal, near, y_edge, outer, sides, gains, row_terms, lat_terms, out, fields, gained
):
    col, gz = position()
    core = gz % 2
    even_col = col % 2 == 0
    lane = iota((1, LATS), 1)
    outer_at = OUTER_ROW - Y_ROW
    beyond = gz + 2 * core - 1
    inside = jnp.where((beyond >= 0) & (beyond < floors), 1.0, 0.0)
    for lon in range(LONS):
        fields[lon] = y_edge[pl.ds(lon, members, stride=LONS), :] * inside
    for lev in range(LEVS):
        fields[outer_at + lev] = outer[lev * members : (lev + 1) * members, :]
    wet = mask[...].astype(F32)
    ocean = [wet[lon : lon + 1] for lon in range(LONS)]
    edge = members * LEVS
    terms = (sides, gains, row_terms, lat_terms)
    move_rows(fields, gained, Y_ROW, EXT_ROWS, ocean + [outer[edge : edge + 1, :]] * LEVS, terms, chunks)

    for r in range(ROWS):
        lev, lon = r // LONS, r % LONS
        x = near[r]
        side = [near[INNER_ROW + lev], fields[outer_at + lev]]
        lon_next = near[r + 1] if lon < LONS - 1 else jnp.where(even_col, side[0], side[1])
        lon_prev = near[r - 1] if lon > 0 else jnp.where(even_col, side[1], side[0])
        lat_next = jnp.where(lane < LATS - 1, pltpu.roll(x, LATS - 1, 1), 0.0)
        lat_prev = jnp.where(lane > 0, pltpu.roll(x, 1, 1), 0.0)
        over = jnp.where(core == 1 - lev, near[CORE_ROW + lon], fields[lon])
        vertical = near[r ^ LONS] + over
        tendency = (
            -0.5 * zonal[r : r + 1, :] * (lon_next - lon_prev)
            + LATERAL_MIX * (lon_next + lon_prev + lat_next + lat_prev - 4.0 * x)
            + VERTICAL_MIX * (vertical - 2.0 * x)
        )
        out[pl.ds(r, members, stride=ROWS), :] = x + ocean[lon] * tendency


def room(mebibytes):
    return pltpu.CompilerParams(vmem_limit_bytes=mebibytes * 1024 * 1024)


def swapped(x, axis, bit):
    return lax.ppermute(x, axis, [(i, i ^ bit) for i in range(lax.axis_size(axis))])


def shifted(x, axis, by):
    count = lax.axis_size(axis)
    return lax.ppermute(x, axis, [(i, (i + by) % count) for i in range(count)])


def local(state, observation_site, obs_count, measured_values, observation_noise, loc_pattern, ocean_mask, zonal_current):
    members = state.shape[0]
    columns = lax.axis_size("col")
    floors = lax.axis_size("gz")
    vmem = pl.BlockSpec(memory_space=pltpu.VMEM)
    smem = pl.BlockSpec(memory_space=pltpu.SMEM)
    height = members + 8
    level = members * LONS
    edge = members * LEVS + 8
    flat = state.reshape(members * ROWS, LATS)

    def like(*lengths):
        return [pltpu.VMEM((length, LATS), F32) for length in lengths]

    kept, given = pl.pallas_call(
        functools.partial(pick_kernel, members, columns),
        out_shape=like(height, height),
        in_specs=[smem] + [vmem] * 6,
        out_specs=[vmem] * 2,
        name="pick_priors",
    )(
        obs_count.reshape(1, BATCHES),
        loc_pattern.reshape(BATCHES, 1, columns),
        observation_site,
        measured_values,
        observation_noise,
        ocean_mask,
        flat,
    )

    mine = kept + swapped(given, "gz", 1)
    core_send, y_send, inner, outer, own = pl.pallas_call(
        functools.partial(edges_kernel, members),
        out_shape=like(level, level, edge, edge) + [pltpu.VMEM((ROWS, members, LATS), F32)],
        in_specs=[vmem] * 2,
        out_specs=[vmem] * 5,
        cost_estimate=pl.CostEstimate(flops=0, bytes_accessed=1 << 22, transcendentals=0),
        name="copy_edges",
    )(ocean_mask, flat)
    core_edge = swapped(core_send, "gz", 1)
    for bit in range(2, floors, 2):
        mine = mine + swapped(mine, "gz", bit)
    flip = columns <= 2 * WINDOW + 1 and columns & (columns - 1) == 0
    if flip:
        inner = swapped(jnp.concatenate([mine, inner]), "col", 1)
        bits = list(range(2, columns, 2))
        passed = [swapped(mine, "col", bit) for bit in bits]
        near = jnp.stack([mine, inner[:height]] + passed)
        gathered = [near, swapped(near[2:], "col", 1)]
        around = [0, 1] + bits + [bit + 1 for bit in bits]
    else:
        inner = swapped(inner, "col", 1)
        around = tuple(range(-WINDOW, WINDOW + 1)) if columns > 2 * WINDOW + 1 else tuple(range(columns))
        gathered = [(mine if by == 0 else shifted(mine, "col", -by))[None] for by in around]

    ends = [(i, i + 1) for i in range(1, floors - 1, 2)]
    ends += [(j, i) for i, j in ends]
    ends += [(i, i) for i in range(floors) if i not in dict(ends)]
    y_edge = lax.ppermute(y_send, "gz", ends)
    ring = [(i, (i + 1) % columns) for i in range(1, columns, 2)]
    outer = lax.ppermute(outer, "col", ring + [(j, i) for i, j in ring])

    parts = tuple(part.shape[0] for part in gathered)
    other = [swapped(part, "gz", 1) for part in gathered]

    slots = min(sum(parts) * CAP, MEAN_COUNT * columns)
    chunks = -(-slots // CHUNK)
    rows = Y_ROW + 2 * chunks
    several = chunks > 1
    count = BATCHES * chunks
    limit = room(48 if several else 16)
    near, *terms = pl.pallas_call(
        functools.partial(near_kernel, members, parts, columns, flip, around, chunks),
        out_shape=[
            pltpu.VMEM((rows, members, LATS), F32),
            pltpu.VMEM((count, CHUNK, CHUNK), BF16),
            pltpu.VMEM((count, 2 * members, CHUNK), BF16),
            pltpu.VMEM((count, CHUNK, LATS), F32),
            pltpu.VMEM((count, CHUNK, LATS), F32),
        ],
        in_specs=[vmem] * (4 + 2 * len(parts)),
        out_specs=[vmem] * 5,
        scratch_shapes=[
            pltpu.VMEM((BATCHES, chunks * CHUNK // CAP, height, CAP), F32),
            pltpu.VMEM((Y_ROW if several else 1, members, LATS), F32),
        ],
        compiler_params=limit,
        cost_estimate=pl.CostEstimate(flops=0, bytes_accessed=0, transcendentals=0),
        name="analyse_near",
    )(ocean_mask, own, core_edge, inner, *gathered, *other)
    out = pl.pallas_call(
        functools.partial(far_kernel, members, columns, floors, chunks),
        out_shape=jax.ShapeDtypeStruct((members * ROWS, LATS), F32),
        in_specs=[vmem] * 9,
        out_specs=vmem,
        scratch_shapes=[
            pltpu.VMEM((EXT_ROWS - Y_ROW, members, LATS), F32),
            pltpu.VMEM((EXT_ROWS - Y_ROW if several else 1, members, LATS), F32),
        ],
        compiler_params=limit,
        name="analyse_far_and_step",
    )(ocean_mask, zonal_current.reshape(ROWS, LATS), near, y_edge, outer, *terms)
    return out.reshape(state.shape)


def solution(mesh):
    in_specs = (
        P(None, "gz", "col", None),
        P(),
        P(None, "col"),
        P(None, "col"),
        P(None, "col"),
        P(None, None, "col"),
        P("col", None),
        P("gz", "col", None),
    )
    out_specs = P(None, "gz", "col", None)
    return jax.shard_map(local, mesh=mesh, in_specs=in_specs, out_specs=out_specs, check_vma=False)
```

```python
import functools

import jax
import jax.numpy as jnp
from jax import lax
from jax.experimental import pallas as pl
from jax.experimental.pallas import tpu as pltpu
from jax.sharding import PartitionSpec as P

LEVS = 2
LONS = 8
LATS = 128
BATCHES = 2
REACH = 3
CAP = 128
MEAN_COUNT = 32
WINDOW = 2 * REACH + 1
CHUNK = 256

CELLS = LEVS * LONS * LATS
ROWS = LEVS * LONS
CORE_ROW = 16
INNER_ROW = 24
Y_ROW = 26
OUTER_ROW = 34
EXT_ROWS = 36
ROW_LIMIT = 40
ROW_COLUMN = 24

LATERAL_MIX = 0.2
VERTICAL_MIX = 0.15

F32 = jnp.float32
BF16 = jnp.bfloat16


def iota(shape, dim):
    return lax.broadcasted_iota(jnp.int32, shape, dim)


def halves(x):
    high = x.astype(BF16)
    return high, (x - high.astype(F32)).astype(BF16)


def dot(a, b):
    return lax.dot_general(a, b, (((1,), (0,)), ((), ())), preferred_element_type=F32)


def dot_lanes(a, b):
    return lax.dot_general(a, b, (((1,), (1,)), ((), ())), preferred_element_type=F32)


def for_each(count, body):
    if count == 1:
        body(0)
    else:
        lax.fori_loop(0, count, lambda i, unused: (body(i), unused)[1], 0)


def rows_of(members):
    names = ("mask", "value", "noise", "links", "site", "occupied", "owner", "count")
    return {name: members + i for i, name in enumerate(names)}


def position():
    return lax.axis_index("col").astype(jnp.int32), lax.axis_index("gz").astype(jnp.int32)


def pick_kernel(members, columns, count, linked, site, value, noise, mask, state, kept, given):
    col, gz = position()
    core = gz % 2
    lane = iota((1, CAP), 1)
    at = pl.multiple_of(col * CAP, CAP)
    index, filled = [], []
    for b in range(BATCHES):
        occupied = lane < count[0, b]
        filled.append(occupied)
        index.append(jnp.where(occupied, site[b : b + 1, pl.ds(at, CAP)] - gz * CELLS, -1))
    wanted = jnp.concatenate(index, 1)
    total = jnp.zeros((3 * members + 16, BATCHES * CAP), F32)
    cell = iota((2 * LATS, BATCHES * CAP), 0)
    ocean = mask[...].astype(F32)
    for pair in range(ROWS // 2):
        left = []
        for r in (2 * pair, 2 * pair + 1):
            x = state[pl.ds(r, members, stride=ROWS), :]
            high = x.astype(BF16)
            rest = x - high.astype(F32)
            middle = rest.astype(BF16)
            low = (rest - middle.astype(F32)).astype(BF16)
            lon = r % LONS
            row = jnp.broadcast_to(ocean[lon : lon + 1, :], (16, LATS)).astype(BF16)
            left.append(jnp.concatenate([high, row, middle, low], 0))
        hit = jnp.where(cell + pair * 2 * LATS == wanted, 1.0, 0.0).astype(BF16)
        total = total + dot(jnp.concatenate(left, 1), hit)
    m = members
    picked = (total[:m] + total[m + 16 : 2 * m + 16]) + total[2 * m + 16 :]
    first = jnp.where(gz == 0, 1.0, 0.0)
    for b in range(BATCHES):
        here = slice(b * CAP, (b + 1) * CAP)
        once = jnp.where(filled[b], first, 0.0)
        links = jnp.concatenate([linked[b].astype(F32), jnp.zeros((1, CAP - columns), F32)], 1)
        tail = [
            total[m : m + 1, here],
            value[b : b + 1, :] * once,
            noise[b : b + 1, :] * once,
            links * first,
            site[b : b + 1, pl.ds(at, CAP)].astype(F32) * once,
            once,
            once * col.astype(F32),
            jnp.full((1, CAP), count[0, b].astype(F32) * first),
        ]
        block = jnp.concatenate([picked[:, here]] + tail, 0)

        @pl.when(core == b)
        def _():
            kept[...] = block

        @pl.when(core != b)
        def _():
            given[...] = block


def edges_kernel(members, mask, state, core_send, y_send, inner, outer, rows):
    col, gz = position()
    core = gz % 2
    ocean = mask[...].astype(F32)
    for r in range(ROWS):
        rows[r] = state[pl.ds(r, members, stride=ROWS), :]
    for member in range(members):
        to = slice(member * LONS, (member + 1) * LONS)
        core_send[to, :] = state[pl.ds(pl.multiple_of(member * ROWS + (1 - core) * LONS, LONS), LONS), :]
        y_send[to, :] = state[pl.ds(pl.multiple_of(member * ROWS + core * LONS, LONS), LONS), :]
    even = col % 2 == 0
    for lev in range(LEVS):
        west, east = rows[lev * LONS], rows[lev * LONS + LONS - 1]
        to = slice(lev * members, (lev + 1) * members)
        inner[to, :] = jnp.where(even, east, west)
        outer[to, :] = jnp.where(even, west, east)
    west = jnp.broadcast_to(ocean[:1], (8, LATS))
    east = jnp.broadcast_to(ocean[LONS - 1 :], (8, LATS))
    inner[LEVS * members :, :] = jnp.where(even, east, west)
    outer[LEVS * members :, :] = jnp.where(even, west, east)


def place_terms(col, gz, columns):
    lon_all = columns * LONS
    odd = gz % 2
    even_col = col % 2 == 0
    at = iota((ROW_LIMIT, 1), 0)
    above, below = LEVS * gz + LEVS, LEVS * gz - 1
    own = at < ROWS
    near = (at >= CORE_ROW) & (at < INNER_ROW)
    far = (at >= Y_ROW) & (at < OUTER_ROW)
    row_lev = LEVS * gz + jnp.where(own, at // LONS, at % LEVS)
    row_lev = jnp.where(near, jnp.where(odd == 0, above, below), row_lev)
    row_lev = jnp.where(far, jnp.where(odd == 0, below, above), row_lev)
    west_lon = (col * LONS + lon_all - 1) % lon_all
    east_lon = (col * LONS + LONS) % lon_all
    inner = (at >= INNER_ROW) & (at < Y_ROW)
    row_lon = col * LONS + jnp.where(far, at - Y_ROW, at % LONS)
    row_lon = jnp.where(inner, jnp.where(even_col, east_lon, west_lon), row_lon)
    row_lon = jnp.where(at >= OUTER_ROW, jnp.where(even_col, west_lon, east_lon), row_lon)
    west_col = (col + columns - 1) % columns
    east_col = (col + 1) % columns
    inner_col = jnp.where(even_col, east_col, west_col)
    outer_col = jnp.where(even_col, west_col, east_col)
    return row_lev.astype(F32), row_lon.astype(F32), inner, at >= OUTER_ROW, inner_col, outer_col


def centred_parts(x):
    x = x - jnp.sum(x, 0, keepdims=True) * (1.0 / x.shape[0])
    high, low = halves(x)
    return jnp.concatenate([high, low, high, jnp.zeros((16, x.shape[1]), BF16)], 0)


def products(covariance, local, gains):
    members = gains.shape[0] // 2
    high, low = halves(covariance * local)
    return dot(gains, high), dot(gains[:members], low)


def added(first, second):
    members = second.shape[0]
    return (first[:members] + first[members:]) + second


def increment(x, sides, gains, local):
    return added(*products(dot(sides, centred_parts(x)), local, gains))


def move_pairs(fields, into, first, last, ocean, terms, steps, meanwhile=None):
    sides, gains, row_part, lat_part = terms
    ahead = []

    def finish():
        t, at, x, covariance = ahead.pop(0)
        columns = [ROW_COLUMN + first + at + h for h in range(2)]
        tapers = [lat_part[t] * row_part[t, :, c : c + 1] for c in columns]
        moved = added(*products(covariance, jnp.concatenate(tapers, 1), gains[t]))
        moved = moved * jnp.concatenate([ocean[at], ocean[at + 1]], 1)
        for h in range(2):
            piece = slice(h * LATS, (h + 1) * LATS)
            if into is fields:
                fields[at + h] = x[:, piece] + moved[:, piece]
            else:
                into[at + h] = into[at + h] + moved[:, piece]

    for i, (t, at) in enumerate([(t, at) for t in steps for at in range(0, last - first, 2)]):
        if meanwhile is not None and i == meanwhile[0]:
            meanwhile[1]()
        if ahead and ahead[0][1] == at:
            finish()
        x = jnp.concatenate([fields[at], fields[at + 1]], 1)
        ahead.append((t, at, x, dot(sides[t], centred_parts(x))))
        if len(ahead) > 1:
            finish()
    while ahead:
        finish()


def move_rows(fields, gained, first, last, ocean, terms, chunks, meanwhile=None):
    if chunks == 1:
        move_pairs(fields, fields, first, last, ocean, terms, range(BATCHES), meanwhile)
        return
    if meanwhile is not None:
        meanwhile[1]()
    for b in range(BATCHES):
        gained[...] = jnp.zeros_like(gained)
        for_each(chunks, lambda k: move_pairs(fields, gained, first, last, ocean, terms, [b * chunks + k]))
        for at in range(last - first):
            fields[at] = fields[at] + gained[at]


def near_kernel(members, parts, columns, floors, flip, around, chunks, mask, own, core_edge, y_edge, inner, *rest):
    mine_parts, other_parts = rest[: len(parts)], rest[len(parts) : 2 * len(parts)]
    fields, sides, gains, row_terms, lat_terms, packed, gained = rest[2 * len(parts) :]
    mine = [part.at[i] for part, size in zip(mine_parts, parts) for i in range(size)]
    other = [part.at[i] for part, size in zip(other_parts, parts) for i in range(size)]
    blocks = len(mine)
    col, gz = position()
    core = gz % 2
    lon_all = columns * LONS
    place = rows_of(members)
    denominator = 1.0 / (members - 1)
    height = members + 8
    owners = [col ^ i if flip else (col + i + columns) % columns for i in around]

    lane = iota((1, LATS), 1)
    pad = (-blocks) % 16
    tables = []
    for b in range(BATCHES):
        start = jnp.zeros((1, CAP), jnp.int32)
        tiles = [jnp.zeros((height, CAP), F32)] * (chunks * CHUNK // CAP)
        links = []
        for j in range(blocks):
            block = jnp.where(core == b, mine[j][...], other[j][...])
            links.append(block[place["links"] : place["links"] + 1, :])
            if j == 0:
                tiles[0] = block
            else:
                shift = start % CAP
                turned = pltpu.roll(block, shift[0, 0], 1)
                into = start // CAP + jnp.where(lane < shift, 1, 0)
                tiles = [tile + jnp.where(into == i, turned, 0.0) for i, tile in enumerate(tiles)]
            start = start + block[place["count"] : place["count"] + 1, :].astype(jnp.int32)
        for i, tile in enumerate(tiles):
            packed[b, i] = tile
        tables.append(jnp.concatenate(links + [jnp.zeros((pad, CAP), F32)] * (pad > 0), 0).astype(BF16))

    inner_start = inner.shape[0] - (members * LEVS + 8)
    for r in range(ROWS):
        fields[r] = own[r]
    level = gz + 2 * core - 1
    beyond = jnp.where((level >= 0) & (level < floors), 1.0, 0.0)
    for lon in range(LONS):
        fields[CORE_ROW + lon] = core_edge[pl.ds(lon, members, stride=LONS), :]
        fields[Y_ROW + lon] = y_edge[pl.ds(lon, members, stride=LONS), :] * beyond
    for lev in range(LEVS):
        at = inner_start + lev * members
        fields[INNER_ROW + lev] = inner[at : at + members, :]
    wet = mask[...].astype(F32)
    ocean = [wet[lon : lon + 1] for lon in range(LONS)] * 3
    at = inner_start + members * LEVS
    ocean += [inner[at : at + 1, :]] * LEVS + ocean[:LONS]

    row_lev, row_lon, inside, outside, inner_col, outer_col = place_terms(col, gz, columns)

    def places(site, owner):
        site = site.astype(jnp.int32)
        lev = site // (LONS * LATS)
        lon = owner.astype(jnp.int32) * LONS + site // LATS % LONS
        return lev.astype(F32), lon.astype(F32), (site % LATS).astype(F32)

    def lon_square(a, b):
        gap = jnp.abs(a - b)
        gap = jnp.minimum(gap, lon_all - gap) * (1.0 / (2.0 * LONS))
        return 1.0 + gap * gap

    def lev_square(a, b):
        gap = (a - b) * 0.5
        return 1.0 + gap * gap

    def lat_square(a, b):
        gap = (a - b) * (1.0 / (LATS // 8))
        return 1.0 + gap * gap

    def slots_of(b, k):
        wide = jnp.concatenate([packed[b, 2 * k], packed[b, 2 * k + 1]], 1)

        def row(name):
            return wide[place[name] : place[name] + 1]

        return wide, row

    def batch_terms(b, k):
        wide, row = slots_of(b, k)
        occupied = row("occupied")
        if b == 0:
            prior = wide[:members]
        else:
            prior = jnp.concatenate([fields[OUTER_ROW + 2 * k], fields[OUTER_ROW + 2 * k + 1]], 1) * occupied
        noise = jnp.where(occupied > 0, row("noise"), 1.0)
        mean = jnp.sum(prior, 0, keepdims=True) / members
        anomaly = prior - mean
        spread = jnp.sum(anomaly * anomaly, 0, keepdims=True) * denominator
        total = spread + noise
        shrink = 1.0 / (1.0 + jnp.sqrt(noise / total))
        gain = ((row("value") - mean) - shrink * anomaly) / total
        high = anomaly.astype(BF16).astype(F32)
        stack = jnp.concatenate([high, high, anomaly - high, jnp.zeros((16, CHUNK), F32)], 0)
        t = b * chunks + k
        sides[t] = stack.T.astype(BF16)
        gains[t] = jnp.concatenate(halves(gain), 0)

    def batch_tapers(b, k):
        wide, row = slots_of(b, k)
        owner = row("owner")
        lev, lon, lat = places(row("site"), owner)
        holder = jnp.where(iota((CAP, CHUNK), 0).astype(F32) == owner, 1.0, 0.0).astype(BF16)
        by_block = dot(tables[b], holder)
        weight = []
        for target in (col, inner_col, outer_col):
            total = jnp.zeros((1, CHUNK), F32)
            for j in range(blocks):
                total = total + jnp.where(owners[j] == target, by_block[j : j + 1], 0.0)
            weight.append(total)
        weight = jnp.where(inside, weight[1], jnp.where(outside, weight[2], weight[0]))
        weight = weight * denominator / (lev_square(row_lev, lev) * lon_square(row_lon, lon))
        spare = LATS - ROW_COLUMN - ROW_LIMIT
        table = jnp.concatenate(
            [lat, lev, lon, jnp.zeros((5, CHUNK), F32), by_block[:16], weight, jnp.zeros((spare, CHUNK), F32)], 0
        )
        t = b * chunks + k
        row_terms[t] = table.T
        lat_terms[t] = 1.0 / lat_square(lane.astype(F32), row_terms[t, :, 0:1])

    def site_weights(k0, k1):
        wide, row = slots_of(1, k1)
        owner = row("owner")
        lev, lon, lat = places(row("site"), owner)
        there = [jnp.where(owner == owners[j].astype(F32), 1.0, 0.0) for j in range(blocks)]
        there += [jnp.zeros((pad, CHUNK), F32)] * (pad > 0)
        weight = dot(row_terms[k0, :, 8:24].astype(BF16), jnp.concatenate(there, 0).astype(BF16))
        lat0, lev0, lon0 = [row_terms[k0, :, i : i + 1] for i in range(3)]
        square = lat_square(lat0, lat) * lon_square(lon0, lon) * lev_square(lev0, lev)
        return weight * denominator / square, wide

    def first_terms(k):
        batch_terms(0, k)
        batch_tapers(0, k)

        def site_chunk(k1):
            taper, wide = site_weights(k, k1)
            x = wide[:members]
            moved = increment(x, sides[k], gains[k], taper) * wide[members : members + 1]
            for h in range(2):
                at = OUTER_ROW + 2 * k1 + h
                piece = slice(h * LATS, (h + 1) * LATS)
                before = x[:, piece] if chunks == 1 else jnp.where(k == 0, x[:, piece], fields[at])
                fields[at] = before + moved[:, piece]

        for_each(chunks, site_chunk)

    def second_terms(k):
        batch_terms(1, k)
        batch_tapers(1, k)

    terms = (sides, gains, row_terms, lat_terms)
    for_each(chunks, first_terms)
    meanwhile = (6, lambda: for_each(chunks, second_terms))
    move_rows(fields, gained, 0, OUTER_ROW, ocean, terms, chunks, meanwhile)


def far_kernel(
    members, columns, chunks, mask, zonal, near, outer, sides, gains, row_terms, lat_terms, out, fields, gained
):
    col, gz = position()
    core = gz % 2
    even_col = col % 2 == 0
    lane = iota((1, LATS), 1)
    outer_at = 0
    for lev in range(LEVS):
        fields[outer_at + lev] = outer[lev * members : (lev + 1) * members, :]
    wet = mask[...].astype(F32)
    ocean = [wet[lon : lon + 1] for lon in range(LONS)]
    edge = members * LEVS
    terms = (sides, gains, row_terms, lat_terms)
    move_rows(fields, gained, OUTER_ROW, EXT_ROWS, [outer[edge : edge + 1, :]] * LEVS, terms, chunks)

    for r in range(ROWS):
        lev, lon = r // LONS, r % LONS
        x = near[r]
        side = [near[INNER_ROW + lev], fields[outer_at + lev]]
        lon_next = near[r + 1] if lon < LONS - 1 else jnp.where(even_col, side[0], side[1])
        lon_prev = near[r - 1] if lon > 0 else jnp.where(even_col, side[1], side[0])
        lat_next = jnp.where(lane < LATS - 1, pltpu.roll(x, LATS - 1, 1), 0.0)
        lat_prev = jnp.where(lane > 0, pltpu.roll(x, 1, 1), 0.0)
        over = jnp.where(core == 1 - lev, near[CORE_ROW + lon], near[Y_ROW + lon])
        vertical = near[r ^ LONS] + over
        tendency = (
            -0.5 * zonal[r : r + 1, :] * (lon_next - lon_prev)
            + LATERAL_MIX * (lon_next + lon_prev + lat_next + lat_prev - 4.0 * x)
            + VERTICAL_MIX * (vertical - 2.0 * x)
        )
        out[pl.ds(r, members, stride=ROWS), :] = x + ocean[lon] * tendency


def room(mebibytes):
    return pltpu.CompilerParams(vmem_limit_bytes=mebibytes * 1024 * 1024)


def swapped(x, axis, bit):
    return lax.ppermute(x, axis, [(i, i ^ bit) for i in range(lax.axis_size(axis))])


def shifted(x, axis, by):
    count = lax.axis_size(axis)
    return lax.ppermute(x, axis, [(i, (i + by) % count) for i in range(count)])


def local(state, observation_site, obs_count, measured_values, observation_noise, loc_pattern, ocean_mask, zonal_current):
    members = state.shape[0]
    columns = lax.axis_size("col")
    floors = lax.axis_size("gz")
    vmem = pl.BlockSpec(memory_space=pltpu.VMEM)
    smem = pl.BlockSpec(memory_space=pltpu.SMEM)
    height = members + 8
    level = members * LONS
    edge = members * LEVS + 8
    flat = state.reshape(members * ROWS, LATS)

    def like(*lengths):
        return [pltpu.VMEM((length, LATS), F32) for length in lengths]

    kept, given = pl.pallas_call(
        functools.partial(pick_kernel, members, columns),
        out_shape=like(height, height),
        in_specs=[smem] + [vmem] * 6,
        out_specs=[vmem] * 2,
        name="pick_priors",
    )(
        obs_count.reshape(1, BATCHES),
        loc_pattern.reshape(BATCHES, 1, columns),
        observation_site,
        measured_values,
        observation_noise,
        ocean_mask,
        flat,
    )

    mine = kept + swapped(given, "gz", 1)
    core_send, y_send, inner, outer, own = pl.pallas_call(
        functools.partial(edges_kernel, members),
        out_shape=like(level, level, edge, edge) + [pltpu.VMEM((ROWS, members, LATS), F32)],
        in_specs=[vmem] * 2,
        out_specs=[vmem] * 5,
        cost_estimate=pl.CostEstimate(flops=0, bytes_accessed=1 << 22, transcendentals=0),
        name="copy_edges",
    )(ocean_mask, flat)
    core_edge = swapped(core_send, "gz", 1)
    for bit in range(2, floors, 2):
        mine = mine + swapped(mine, "gz", bit)
    flip = columns <= 2 * WINDOW + 1 and columns & (columns - 1) == 0
    if flip:
        inner = swapped(jnp.concatenate([mine, inner]), "col", 1)
        bits = list(range(2, columns, 2))
        passed = [swapped(mine, "col", bit) for bit in bits]
        near = jnp.stack([mine, inner[:height]] + passed)
        gathered = [near, swapped(near[2:], "col", 1)]
        around = [0, 1] + bits + [bit + 1 for bit in bits]
    else:
        inner = swapped(inner, "col", 1)
        around = tuple(range(-WINDOW, WINDOW + 1)) if columns > 2 * WINDOW + 1 else tuple(range(columns))
        gathered = [(mine if by == 0 else shifted(mine, "col", -by))[None] for by in around]

    ends = [(i, i + 1) for i in range(1, floors - 1, 2)]
    ends += [(j, i) for i, j in ends]
    ends += [(i, i) for i in range(floors) if i not in dict(ends)]
    y_edge = lax.ppermute(y_send, "gz", ends)
    ring = [(i, (i + 1) % columns) for i in range(1, columns, 2)]
    outer = lax.ppermute(outer, "col", ring + [(j, i) for i, j in ring])

    parts = tuple(part.shape[0] for part in gathered)
    other = [swapped(part, "gz", 1) for part in gathered]

    slots = min(sum(parts) * CAP, MEAN_COUNT * columns)
    chunks = -(-slots // CHUNK)
    rows = OUTER_ROW + 2 * chunks
    several = chunks > 1
    count = BATCHES * chunks
    limit = room(48 if several else 16)
    near, *terms = pl.pallas_call(
        functools.partial(near_kernel, members, parts, columns, floors, flip, around, chunks),
        out_shape=[
            pltpu.VMEM((rows, members, LATS), F32),
            pltpu.VMEM((count, CHUNK, CHUNK), BF16),
            pltpu.VMEM((count, 2 * members, CHUNK), BF16),
            pltpu.VMEM((count, CHUNK, LATS), F32),
            pltpu.VMEM((count, CHUNK, LATS), F32),
        ],
        in_specs=[vmem] * (5 + 2 * len(parts)),
        out_specs=[vmem] * 5,
        scratch_shapes=[
            pltpu.VMEM((BATCHES, chunks * CHUNK // CAP, height, CAP), F32),
            pltpu.VMEM((OUTER_ROW if several else 1, members, LATS), F32),
        ],
        compiler_params=limit,
        cost_estimate=pl.CostEstimate(flops=0, bytes_accessed=0, transcendentals=0),
        name="analyse_near",
    )(ocean_mask, own, core_edge, y_edge.reshape(level, LATS), inner, *gathered, *other)
    out = pl.pallas_call(
        functools.partial(far_kernel, members, columns, chunks),
        out_shape=jax.ShapeDtypeStruct((members * ROWS, LATS), F32),
        in_specs=[vmem] * 8,
        out_specs=vmem,
        scratch_shapes=[
            pltpu.VMEM((EXT_ROWS - OUTER_ROW, members, LATS), F32),
            pltpu.VMEM((EXT_ROWS - OUTER_ROW if several else 1, members, LATS), F32),
        ],
        compiler_params=limit,
        name="analyse_far_and_step",
    )(ocean_mask, zonal_current.reshape(ROWS, LATS), near, outer, *terms)
    return out.reshape(state.shape)


def solution(mesh):
    in_specs = (
        P(None, "gz", "col", None),
        P(),
        P(None, "col"),
        P(None, "col"),
        P(None, "col"),
        P(None, None, "col"),
        P("col", None),
        P("gz", "col", None),
    )
    out_specs = P(None, "gz", "col", None)
    return jax.shard_map(local, mesh=mesh, in_specs=in_specs, out_specs=out_specs, check_vma=False)
```

```python
import functools

import jax
import jax.numpy as jnp
from jax import lax
from jax.experimental import pallas as pl
from jax.experimental.pallas import tpu as pltpu
from jax.sharding import PartitionSpec as P

LEVS = 2
LONS = 8
LATS = 128
BATCHES = 2
REACH = 3
CAP = 128
MEAN_COUNT = 32
WINDOW = 2 * REACH + 1
CHUNK = 256

CELLS = LEVS * LONS * LATS
ROWS = LEVS * LONS
CORE_ROW = 16
INNER_ROW = 24
Y_ROW = 26
OUTER_ROW = 34
EXT_ROWS = 36
ROW_LIMIT = 40
ROW_COLUMN = 24

LATERAL_MIX = 0.2
VERTICAL_MIX = 0.15

F32 = jnp.float32
BF16 = jnp.bfloat16


def iota(shape, dim):
    return lax.broadcasted_iota(jnp.int32, shape, dim)


def halves(x):
    high = x.astype(BF16)
    return high, (x - high.astype(F32)).astype(BF16)


def dot(a, b):
    return lax.dot_general(a, b, (((1,), (0,)), ((), ())), preferred_element_type=F32)


def dot_lanes(a, b):
    return lax.dot_general(a, b, (((1,), (1,)), ((), ())), preferred_element_type=F32)


def for_each(count, body):
    if count == 1:
        body(0)
    else:
        lax.fori_loop(0, count, lambda i, unused: (body(i), unused)[1], 0)


def rows_of(members):
    names = ("mask", "value", "noise", "links", "site", "occupied", "owner", "count")
    return {name: members + i for i, name in enumerate(names)}


def position():
    return lax.axis_index("col").astype(jnp.int32), lax.axis_index("gz").astype(jnp.int32)


def pick_kernel(members, columns, count, linked, site, value, noise, mask, state, kept, given):
    col, gz = position()
    core = gz % 2
    lane = iota((1, CAP), 1)
    at = pl.multiple_of(col * CAP, CAP)
    index, filled = [], []
    for b in range(BATCHES):
        occupied = lane < count[0, b]
        filled.append(occupied)
        index.append(jnp.where(occupied, site[b : b + 1, pl.ds(at, CAP)] - gz * CELLS, -1))
    wanted = jnp.concatenate(index, 1)
    total = jnp.zeros((3 * members + 16, BATCHES * CAP), F32)
    cell = iota((2 * LATS, BATCHES * CAP), 0)
    ocean = mask[...].astype(F32)
    for pair in range(ROWS // 2):
        left = []
        for r in (2 * pair, 2 * pair + 1):
            x = state[pl.ds(r, members, stride=ROWS), :]
            high = x.astype(BF16)
            rest = x - high.astype(F32)
            middle = rest.astype(BF16)
            low = (rest - middle.astype(F32)).astype(BF16)
            lon = r % LONS
            row = jnp.broadcast_to(ocean[lon : lon + 1, :], (16, LATS)).astype(BF16)
            left.append(jnp.concatenate([high, row, middle, low], 0))
        hit = jnp.where(cell + pair * 2 * LATS == wanted, 1.0, 0.0).astype(BF16)
        total = total + dot(jnp.concatenate(left, 1), hit)
    m = members
    picked = (total[:m] + total[m + 16 : 2 * m + 16]) + total[2 * m + 16 :]
    first = jnp.where(gz == 0, 1.0, 0.0)
    for b in range(BATCHES):
        here = slice(b * CAP, (b + 1) * CAP)
        once = jnp.where(filled[b], first, 0.0)
        links = jnp.concatenate([linked[b].astype(F32), jnp.zeros((1, CAP - columns), F32)], 1)
        tail = [
            total[m : m + 1, here],
            value[b : b + 1, :] * once,
            noise[b : b + 1, :] * once,
            links * first,
            site[b : b + 1, pl.ds(at, CAP)].astype(F32) * once,
            once,
            once * col.astype(F32),
            jnp.full((1, CAP), count[0, b].astype(F32) * first),
        ]
        block = jnp.concatenate([picked[:, here]] + tail, 0)

        @pl.when(core == b)
        def _():
            kept[...] = block

        @pl.when(core != b)
        def _():
            given[...] = block


def edges_kernel(members, mask, state, core_send, y_send, inner, outer, rows):
    col, gz = position()
    core = gz % 2
    ocean = mask[...].astype(F32)
    for r in range(ROWS):
        rows[r] = state[pl.ds(r, members, stride=ROWS), :]
    for member in range(members):
        to = slice(member * LONS, (member + 1) * LONS)
        core_send[to, :] = state[pl.ds(pl.multiple_of(member * ROWS + (1 - core) * LONS, LONS), LONS), :]
        y_send[to, :] = state[pl.ds(pl.multiple_of(member * ROWS + core * LONS, LONS), LONS), :]
    even = col % 2 == 0
    for lev in range(LEVS):
        west, east = rows[lev * LONS], rows[lev * LONS + LONS - 1]
        to = slice(lev * members, (lev + 1) * members)
        inner[to, :] = jnp.where(even, east, west)
        outer[to, :] = jnp.where(even, west, east)
    west = jnp.broadcast_to(ocean[:1], (8, LATS))
    east = jnp.broadcast_to(ocean[LONS - 1 :], (8, LATS))
    inner[LEVS * members :, :] = jnp.where(even, east, west)
    outer[LEVS * members :, :] = jnp.where(even, west, east)


def place_terms(col, gz, columns):
    lon_all = columns * LONS
    odd = gz % 2
    even_col = col % 2 == 0
    at = iota((ROW_LIMIT, 1), 0)
    above, below = LEVS * gz + LEVS, LEVS * gz - 1
    own = at < ROWS
    near = (at >= CORE_ROW) & (at < INNER_ROW)
    far = (at >= Y_ROW) & (at < OUTER_ROW)
    row_lev = LEVS * gz + jnp.where(own, at // LONS, at % LEVS)
    row_lev = jnp.where(near, jnp.where(odd == 0, above, below), row_lev)
    row_lev = jnp.where(far, jnp.where(odd == 0, below, above), row_lev)
    west_lon = (col * LONS + lon_all - 1) % lon_all
    east_lon = (col * LONS + LONS) % lon_all
    inner = (at >= INNER_ROW) & (at < Y_ROW)
    row_lon = col * LONS + jnp.where(far, at - Y_ROW, at % LONS)
    row_lon = jnp.where(inner, jnp.where(even_col, east_lon, west_lon), row_lon)
    row_lon = jnp.where(at >= OUTER_ROW, jnp.where(even_col, west_lon, east_lon), row_lon)
    west_col = (col + columns - 1) % columns
    east_col = (col + 1) % columns
    inner_col = jnp.where(even_col, east_col, west_col)
    outer_col = jnp.where(even_col, west_col, east_col)
    return row_lev.astype(F32), row_lon.astype(F32), inner, at >= OUTER_ROW, inner_col, outer_col


def centred_parts(x):
    x = x - jnp.sum(x, 0, keepdims=True) * (1.0 / x.shape[0])
    high, low = halves(x)
    return jnp.concatenate([high, low, high, jnp.zeros((16, x.shape[1]), BF16)], 0)


def products(covariance, local, gains):
    members = gains.shape[0] // 2
    high, low = halves(covariance * local)
    return dot(gains, high), dot(gains[:members], low)


def added(first, second):
    members = second.shape[0]
    return (first[:members] + first[members:]) + second


def increment(x, sides, gains, local):
    return added(*products(dot(sides, centred_parts(x)), local, gains))


def move_pairs(fields, into, first, last, ocean, terms, steps, meanwhile=None, aside=None):
    sides, gains, row_part, lat_part = terms
    ahead = []

    def finish():
        t, at, x, covariance = ahead.pop(0)
        columns = [ROW_COLUMN + first + at + h for h in range(2)]
        tapers = [lat_part[t] * row_part[t, :, c : c + 1] for c in columns]
        parts = products(covariance, jnp.concatenate(tapers, 1), gains[t])
        if aside is not None:
            aside()
        moved = added(*parts) * jnp.concatenate([ocean[at], ocean[at + 1]], 1)
        for h in range(2):
            piece = slice(h * LATS, (h + 1) * LATS)
            if into is fields:
                fields[at + h] = x[:, piece] + moved[:, piece]
            else:
                into[at + h] = into[at + h] + moved[:, piece]

    for i, (t, at) in enumerate([(t, at) for t in steps for at in range(0, last - first, 2)]):
        if meanwhile is not None and i == meanwhile[0]:
            meanwhile[1]()
        if ahead and ahead[0][1] == at:
            finish()
        x = jnp.concatenate([fields[at], fields[at + 1]], 1)
        ahead.append((t, at, x, dot(sides[t], centred_parts(x))))
        if aside is not None:
            aside()
        if len(ahead) > 1:
            finish()
    while ahead:
        finish()


def move_rows(fields, gained, first, last, ocean, terms, chunks, meanwhile=None, aside=None):
    if chunks == 1:
        move_pairs(fields, fields, first, last, ocean, terms, range(BATCHES), meanwhile, aside)
        return
    if meanwhile is not None:
        meanwhile[1]()
    for b in range(BATCHES):
        gained[...] = jnp.zeros_like(gained)
        for_each(chunks, lambda k: move_pairs(fields, gained, first, last, ocean, terms, [b * chunks + k]))
        for at in range(last - first):
            fields[at] = fields[at] + gained[at]


def near_kernel(members, parts, columns, floors, flip, around, chunks, mask, own, core_edge, y_edge, inner, *rest):
    mine_parts, other_parts = rest[: len(parts)], rest[len(parts) : 2 * len(parts)]
    fields, sides, gains, row_terms, lat_terms, packed, gained = rest[2 * len(parts) :]
    mine = [part.at[i] for part, size in zip(mine_parts, parts) for i in range(size)]
    other = [part.at[i] for part, size in zip(other_parts, parts) for i in range(size)]
    blocks = len(mine)
    col, gz = position()
    core = gz % 2
    lon_all = columns * LONS
    place = rows_of(members)
    denominator = 1.0 / (members - 1)
    height = members + 8
    owners = [col ^ i if flip else (col + i + columns) % columns for i in around]

    lane = iota((1, LATS), 1)
    pad = (-blocks) % 16
    tables = []
    for b in range(BATCHES):
        start = jnp.zeros((1, CAP), jnp.int32)
        tiles = [jnp.zeros((height, CAP), F32)] * (chunks * CHUNK // CAP)
        links = []
        for j in range(blocks):
            block = jnp.where(core == b, mine[j][...], other[j][...])
            links.append(block[place["links"] : place["links"] + 1, :])
            if j == 0:
                tiles[0] = block
            else:
                shift = start % CAP
                turned = pltpu.roll(block, shift[0, 0], 1)
                into = start // CAP + jnp.where(lane < shift, 1, 0)
                tiles = [tile + jnp.where(into == i, turned, 0.0) for i, tile in enumerate(tiles)]
            start = start + block[place["count"] : place["count"] + 1, :].astype(jnp.int32)
        for i, tile in enumerate(tiles):
            packed[b, i] = tile
        tables.append(jnp.concatenate(links + [jnp.zeros((pad, CAP), F32)] * (pad > 0), 0).astype(BF16))

    inner_start = inner.shape[0] - (members * LEVS + 8)
    for r in range(ROWS):
        fields[r] = own[r]
    level = gz + 2 * core - 1
    beyond = jnp.where((level >= 0) & (level < floors), 1.0, 0.0)
    for lon in range(LONS):
        fields[CORE_ROW + lon] = core_edge[pl.ds(lon, members, stride=LONS), :]
        fields[Y_ROW + lon] = y_edge[pl.ds(lon, members, stride=LONS), :] * beyond
    for lev in range(LEVS):
        at = inner_start + lev * members
        fields[INNER_ROW + lev] = inner[at : at + members, :]
    wet = mask[...].astype(F32)
    ocean = [wet[lon : lon + 1] for lon in range(LONS)] * 3
    at = inner_start + members * LEVS
    ocean += [inner[at : at + 1, :]] * LEVS + ocean[:LONS]

    row_lev, row_lon, inside, outside, inner_col, outer_col = place_terms(col, gz, columns)

    def places(site, owner):
        site = site.astype(jnp.int32)
        lev = site // (LONS * LATS)
        lon = owner.astype(jnp.int32) * LONS + site // LATS % LONS
        return lev.astype(F32), lon.astype(F32), (site % LATS).astype(F32)

    def lon_square(a, b):
        gap = jnp.abs(a - b)
        gap = jnp.minimum(gap, lon_all - gap) * (1.0 / (2.0 * LONS))
        return 1.0 + gap * gap

    def lev_square(a, b):
        gap = (a - b) * 0.5
        return 1.0 + gap * gap

    def lat_square(a, b):
        gap = (a - b) * (1.0 / (LATS // 8))
        return 1.0 + gap * gap

    def slots_of(b, k):
        wide = jnp.concatenate([packed[b, 2 * k], packed[b, 2 * k + 1]], 1)

        def row(name):
            return wide[place[name] : place[name] + 1]

        return wide, row

    def batch_terms(b, k):
        wide, row = slots_of(b, k)
        occupied = row("occupied")
        if b == 0:
            prior = wide[:members]
        else:
            prior = jnp.concatenate([fields[OUTER_ROW + 2 * k], fields[OUTER_ROW + 2 * k + 1]], 1) * occupied
        noise = jnp.where(occupied > 0, row("noise"), 1.0)
        mean = jnp.sum(prior, 0, keepdims=True) / members
        anomaly = prior - mean
        spread = jnp.sum(anomaly * anomaly, 0, keepdims=True) * denominator
        total = spread + noise
        shrink = 1.0 / (1.0 + jnp.sqrt(noise / total))
        gain = ((row("value") - mean) - shrink * anomaly) / total
        high = anomaly.astype(BF16).astype(F32)
        stack = jnp.concatenate([high, high, anomaly - high, jnp.zeros((16, CHUNK), F32)], 0)
        t = b * chunks + k
        sides[t] = stack.T.astype(BF16)
        gains[t] = jnp.concatenate(halves(gain), 0)

    def batch_tapers(b, k):
        wide, row = slots_of(b, k)
        owner = row("owner")
        lev, lon, lat = places(row("site"), owner)
        holder = jnp.where(iota((CAP, CHUNK), 0).astype(F32) == owner, 1.0, 0.0).astype(BF16)
        by_block = dot(tables[b], holder)
        weight = []
        for target in (col, inner_col, outer_col):
            total = jnp.zeros((1, CHUNK), F32)
            for j in range(blocks):
                total = total + jnp.where(owners[j] == target, by_block[j : j + 1], 0.0)
            weight.append(total)
        weight = jnp.where(inside, weight[1], jnp.where(outside, weight[2], weight[0]))
        weight = weight * denominator / (lev_square(row_lev, lev) * lon_square(row_lon, lon))
        spare = LATS - ROW_COLUMN - ROW_LIMIT
        table = jnp.concatenate(
            [lat, lev, lon, jnp.zeros((5, CHUNK), F32), by_block[:16], weight, jnp.zeros((spare, CHUNK), F32)], 0
        )
        t = b * chunks + k
        row_terms[t] = table.T
        lat_terms[t] = 1.0 / lat_square(lane.astype(F32), row_terms[t, :, 0:1])

    def site_weights(k0, k1):
        wide, row = slots_of(1, k1)
        owner = row("owner")
        lev, lon, lat = places(row("site"), owner)
        there = [jnp.where(owner == owners[j].astype(F32), 1.0, 0.0) for j in range(blocks)]
        there += [jnp.zeros((pad, CHUNK), F32)] * (pad > 0)
        weight = dot(row_terms[k0, :, 8:24].astype(BF16), jnp.concatenate(there, 0).astype(BF16))
        lat0, lev0, lon0 = [row_terms[k0, :, i : i + 1] for i in range(3)]
        square = lat_square(lat0, lat) * lon_square(lon0, lon) * lev_square(lev0, lev)
        return weight * denominator / square, wide

    def first_terms(k):
        batch_terms(0, k)
        batch_tapers(0, k)

        def site_chunk(k1):
            taper, wide = site_weights(k, k1)
            x = wide[:members]
            moved = increment(x, sides[k], gains[k], taper) * wide[members : members + 1]
            for h in range(2):
                at = OUTER_ROW + 2 * k1 + h
                piece = slice(h * LATS, (h + 1) * LATS)
                before = x[:, piece] if chunks == 1 else jnp.where(k == 0, x[:, piece], fields[at])
                fields[at] = before + moved[:, piece]

        for_each(chunks, site_chunk)

    def second_terms(k):
        batch_terms(1, k)
        batch_tapers(1, k)

    terms = (sides, gains, row_terms, lat_terms)
    for_each(chunks, first_terms)
    meanwhile = (6, lambda: for_each(chunks, second_terms))
    move_rows(fields, gained, 0, OUTER_ROW, ocean, terms, chunks, meanwhile)


def far_kernel(
    members, columns, chunks, mask, zonal, near, outer, sides, gains, row_terms, lat_terms, out, fields, gained
):
    col, gz = position()
    core = gz % 2
    even_col = col % 2 == 0
    lane = iota((1, LATS), 1)
    outer_at = 0
    for lev in range(LEVS):
        fields[outer_at + lev] = outer[lev * members : (lev + 1) * members, :]
    wet = mask[...].astype(F32)
    ocean = [wet[lon : lon + 1] for lon in range(LONS)]
    edge = members * LEVS
    terms = (sides, gains, row_terms, lat_terms)
    def step(r):
        lev, lon = r // LONS, r % LONS
        x = near[r]
        side = [near[INNER_ROW + lev], fields[outer_at + lev]]
        lon_next = near[r + 1] if lon < LONS - 1 else jnp.where(even_col, side[0], side[1])
        lon_prev = near[r - 1] if lon > 0 else jnp.where(even_col, side[1], side[0])
        lat_next = jnp.where(lane < LATS - 1, pltpu.roll(x, LATS - 1, 1), 0.0)
        lat_prev = jnp.where(lane > 0, pltpu.roll(x, 1, 1), 0.0)
        over = jnp.where(core == 1 - lev, near[CORE_ROW + lon], near[Y_ROW + lon])
        vertical = near[r ^ LONS] + over
        tendency = (
            -0.5 * zonal[r : r + 1, :] * (lon_next - lon_prev)
            + LATERAL_MIX * (lon_next + lon_prev + lat_next + lat_prev - 4.0 * x)
            + VERTICAL_MIX * (vertical - 2.0 * x)
        )
        out[pl.ds(r, members, stride=ROWS), :] = x + ocean[lon] * tendency

    inside = [r for r in range(ROWS) if 0 < r % LONS < LONS - 1]
    left = list(inside)

    def some_rows():
        for r in left[:3]:
            step(r)
        del left[:3]

    wet_edge = [outer[edge : edge + 1, :]] * LEVS
    move_rows(fields, gained, OUTER_ROW, EXT_ROWS, wet_edge, terms, chunks, aside=some_rows)
    for r in left + [r for r in range(ROWS) if r not in inside]:
        step(r)


def room(mebibytes):
    return pltpu.CompilerParams(vmem_limit_bytes=mebibytes * 1024 * 1024)


def swapped(x, axis, bit):
    return lax.ppermute(x, axis, [(i, i ^ bit) for i in range(lax.axis_size(axis))])


def shifted(x, axis, by):
    count = lax.axis_size(axis)
    return lax.ppermute(x, axis, [(i, (i + by) % count) for i in range(count)])


def local(state, observation_site, obs_count, measured_values, observation_noise, loc_pattern, ocean_mask, zonal_current):
    members = state.shape[0]
    columns = lax.axis_size("col")
    floors = lax.axis_size("gz")
    vmem = pl.BlockSpec(memory_space=pltpu.VMEM)
    smem = pl.BlockSpec(memory_space=pltpu.SMEM)
    height = members + 8
    level = members * LONS
    edge = members * LEVS + 8
    flat = state.reshape(members * ROWS, LATS)

    def like(*lengths):
        return [pltpu.VMEM((length, LATS), F32) for length in lengths]

    kept, given = pl.pallas_call(
        functools.partial(pick_kernel, members, columns),
        out_shape=like(height, height),
        in_specs=[smem] + [vmem] * 6,
        out_specs=[vmem] * 2,
        name="pick_priors",
    )(
        obs_count.reshape(1, BATCHES),
        loc_pattern.reshape(BATCHES, 1, columns),
        observation_site,
        measured_values,
        observation_noise,
        ocean_mask,
        flat,
    )

    mine = kept + swapped(given, "gz", 1)
    core_send, y_send, inner, outer, own = pl.pallas_call(
        functools.partial(edges_kernel, members),
        out_shape=like(level, level, edge, edge) + [pltpu.VMEM((ROWS, members, LATS), F32)],
        in_specs=[vmem] * 2,
        out_specs=[vmem] * 5,
        cost_estimate=pl.CostEstimate(flops=0, bytes_accessed=1 << 22, transcendentals=0),
        name="copy_edges",
    )(ocean_mask, flat)
    core_edge = swapped(core_send, "gz", 1)
    for bit in range(2, floors, 2):
        mine = mine + swapped(mine, "gz", bit)
    flip = columns <= 2 * WINDOW + 1 and columns & (columns - 1) == 0
    if flip:
        inner = swapped(jnp.concatenate([mine, inner]), "col", 1)
        bits = list(range(columns - 2, 0, -2))
        passed = [swapped(mine, "col", bit) for bit in bits]
        near = jnp.stack([mine, inner[:height]] + passed)
        gathered = [near, swapped(near[2:], "col", 1)]
        around = [0, 1] + bits + [bit + 1 for bit in bits]
    else:
        inner = swapped(inner, "col", 1)
        around = tuple(range(-WINDOW, WINDOW + 1)) if columns > 2 * WINDOW + 1 else tuple(range(columns))
        gathered = [(mine if by == 0 else shifted(mine, "col", -by))[None] for by in around]

    ends = [(i, i + 1) for i in range(1, floors - 1, 2)]
    ends += [(j, i) for i, j in ends]
    ends += [(i, i) for i in range(floors) if i not in dict(ends)]
    y_edge = lax.ppermute(y_send, "gz", ends)
    ring = [(i, (i + 1) % columns) for i in range(1, columns, 2)]
    outer = lax.ppermute(outer, "col", ring + [(j, i) for i, j in ring])

    parts = tuple(part.shape[0] for part in gathered)
    other = [swapped(part, "gz", 1) for part in gathered]

    slots = min(sum(parts) * CAP, MEAN_COUNT * columns)
    chunks = -(-slots // CHUNK)
    rows = OUTER_ROW + 2 * chunks
    several = chunks > 1
    count = BATCHES * chunks
    limit = room(48 if several else 16)
    near, *terms = pl.pallas_call(
        functools.partial(near_kernel, members, parts, columns, floors, flip, around, chunks),
        out_shape=[
            pltpu.VMEM((rows, members, LATS), F32),
            pltpu.VMEM((count, CHUNK, CHUNK), BF16),
            pltpu.VMEM((count, 2 * members, CHUNK), BF16),
            pltpu.VMEM((count, CHUNK, LATS), F32),
            pltpu.VMEM((count, CHUNK, LATS), F32),
        ],
        in_specs=[vmem] * (5 + 2 * len(parts)),
        out_specs=[vmem] * 5,
        scratch_shapes=[
            pltpu.VMEM((BATCHES, chunks * CHUNK // CAP, height, CAP), F32),
            pltpu.VMEM((OUTER_ROW if several else 1, members, LATS), F32),
        ],
        compiler_params=limit,
        cost_estimate=pl.CostEstimate(flops=0, bytes_accessed=0, transcendentals=0),
        name="analyse_near",
    )(ocean_mask, own, core_edge, y_edge.reshape(level, LATS), inner, *gathered, *other)
    out = pl.pallas_call(
        functools.partial(far_kernel, members, columns, chunks),
        out_shape=jax.ShapeDtypeStruct((members * ROWS, LATS), F32),
        in_specs=[vmem] * 8,
        out_specs=vmem,
        scratch_shapes=[
            pltpu.VMEM((EXT_ROWS - OUTER_ROW, members, LATS), F32),
            pltpu.VMEM((EXT_ROWS - OUTER_ROW if several else 1, members, LATS), F32),
        ],
        compiler_params=limit,
        name="analyse_far_and_step",
    )(ocean_mask, zonal_current.reshape(ROWS, LATS), near, outer, *terms)
    return out.reshape(state.shape)


def solution(mesh):
    in_specs = (
        P(None, "gz", "col", None),
        P(),
        P(None, "col"),
        P(None, "col"),
        P(None, "col"),
        P(None, None, "col"),
        P("col", None),
        P("gz", "col", None),
    )
    out_specs = P(None, "gz", "col", None)
    return jax.shard_map(local, mesh=mesh, in_specs=in_specs, out_specs=out_specs, check_vma=False)
```
